128 devices in a mesh: hst: 32 (over z, x, core), tensor: 4 (over y).
Axes of the slice: x: 4, y: 4, z: 4, core: 2. Of those that a mesh axis runs over, the one named last changes fastest.
Arguments:
- context_queries: bfloat16 [32768, 8192], P('hst', 'tensor'), may hold values from -64 to 64
- context_keys: bfloat16 [32768, 1024], P('hst', 'tensor'), may hold values from -8 to 8
- context_values: bfloat16 [32768, 1024], P('hst', 'tensor'), may hold values from -6 to 6
- query_token_queries: bfloat16 [256, 8192], P('hst', 'tensor'), may hold values from -64 to 64
- query_token_keys: bfloat16 [256, 1024], P('hst', 'tensor'), may hold values from -8 to 8
- query_token_values: bfloat16 [256, 1024], P('hst', 'tensor'), may hold values from -6 to 6
- out_weight: bfloat16 [8192, 8192], P('tensor', 'hst'), may hold values from -0.0625 to 0.0625
- block_lengths: int32 [32], replicated, may hold values from 1 to 1024, 24576 in all
Outputs:
- context_out: bfloat16 [32768, 8192], P('hst', 'tensor')
- query_out: bfloat16 [256, 8192], P('tensor', 'hst')
The draws below stay inside these ranges and needn't reach their ends.
Inputs may be any that keep to these rules, and one draw needn't show every extreme that they name: `block_lengths`: together the blocks hold 24576 valid positions; at least one block is full.
All inputs are finite; a program needn't handle non-finite values.
Results may differ from the reference program's by a relative error of at most 0.0053.
Values may be sent and summed in bfloat16 or wider, within the bound.
No kernel may reach another device: no remote copies, remote signals or barrier semaphores. Data moves between devices by JAX's collectives and lax.ppermute only.
A program may use at most 128 MiB of HBM per device.

```python
import math
import jax
import jax.numpy as jnp
import numpy as np
from jax import lax

D = 8192
QUERY_HEADS = 64
KEY_VALUE_HEADS = 8
HEAD_DIMENSION = 128
BLOCK_POSITIONS = 1024
QUERY_LENGTH = 256
CONTEXT_LENGTH = 32768
QS = 8
N_HST = 32


def key_offset(key, rows, width, tag):
    folded = jax.random.fold_in(key, tag)
    return 1.6 * jnp.clip(jax.random.normal(folded, (rows, width), jnp.float32), -4.5, 4.5)


def draw_context_keys(key, part):
    base_offset = key_offset(key, CONTEXT_LENGTH, KEY_VALUE_HEADS * HEAD_DIMENSION, 101)
    return base_offset.astype(jnp.bfloat16)


def draw_context_queries(key, part):
    key = jax.random.fold_in(key, 2)
    values = jnp.clip(jax.random.normal(key, (CONTEXT_LENGTH, QUERY_HEADS * HEAD_DIMENSION), jnp.float32), -4.5, 4.5)
    return values.astype(jnp.bfloat16)


def draw_query_token_keys(key, part):
    base_offset = key_offset(key, QUERY_LENGTH, KEY_VALUE_HEADS * HEAD_DIMENSION, 202)
    return base_offset.astype(jnp.bfloat16)


def draw_query_token_queries(key, part):
    key = jax.random.fold_in(key, 4)
    values = jnp.clip(jax.random.normal(key, (QUERY_LENGTH, QUERY_HEADS * HEAD_DIMENSION), jnp.float32), -4.5, 4.5)
    return values.astype(jnp.bfloat16)


def levels(own_key, extent, split, least, largest):
    gain = 1.0
    for axis_at, blocks in split:
        draws = jax.random.uniform(jax.random.fold_in(jax.random.fold_in(own_key, 6), axis_at), (blocks,), jnp.float32, least / len(split), largest / len(split))
        gain = gain * jnp.repeat(jnp.exp(draws), extent[axis_at] // blocks).reshape((-1,) + (1,) * (len(extent) - 1 - axis_at))
    return gain


def length_profile(count, total, most, skew):
    weights = [(1 << 20) // math.isqrt(rank ** skew) + 1 for rank in range(2, count + 1)]
    rest, counts = total - most - (count - 1), [1] * (count - 1)
    while rest > 0:
        candidates = [i for i in range(count - 1) if counts[i] < most]
        pool, budget = sum([weights[i] for i in candidates]), rest
        for i in candidates:
            extra = min(most - counts[i], max(1, budget * weights[i] // pool), rest)
            counts[i] = counts[i] + extra
            rest = rest - extra
    return np.array([most] + counts)


def uneven(rng, number_of, total, bound, skew):
    if number_of == 2:
        one = jax.random.randint(rng, (), max(1, total - bound), min(bound, total - 1) + 1)
        return jnp.stack([one, total - one])
    tallies = jnp.asarray(length_profile(number_of, total, bound, skew), jnp.int32)
    twos = (number_of - 1) // 2
    donor, taker = tallies[1:1 + 2 * twos:2], tallies[2:2 + 2 * twos:2]
    room = jnp.minimum(donor - 1, bound - taker)
    moved = jax.random.randint(jax.random.fold_in(rng, 1), (twos,), 0, 1 << 20) % (room + 1)
    tallies = tallies.at[1:1 + 2 * twos:2].set(donor - moved).at[2:2 + 2 * twos:2].set(taker + moved)
    return tallies[jax.random.permutation(jax.random.fold_in(rng, 2), number_of)]


def scatter_about(key, extent, deviation, bound, pieces=(), kind=jnp.bfloat16):
    values = deviation * jax.random.normal(key, extent, jnp.float32)
    if pieces:
        values = values * levels(key, extent, pieces, -0.22, 0.18)
    return jnp.clip(values, -bound, bound).astype(kind)


def setup_inputs(seed: int = 0) -> dict:
    splits = jax.random.split(jax.random.key(seed), 9)
    return {
        "context_queries": draw_context_queries(jax.random.fold_in(splits[8], 71), 0),
        "context_keys": draw_context_keys(jax.random.fold_in(splits[8], 71), 0),
        "context_values": scatter_about(splits[2], (CONTEXT_LENGTH, KEY_VALUE_HEADS * HEAD_DIMENSION), 1.0, 6.0, ((0, 32), (1, 4))),
        "query_token_queries": draw_query_token_queries(jax.random.fold_in(splits[8], 71), 0),
        "query_token_keys": draw_query_token_keys(jax.random.fold_in(splits[8], 71), 0),
        "query_token_values": scatter_about(splits[5], (QUERY_LENGTH, KEY_VALUE_HEADS * HEAD_DIMENSION), 1.0, 6.0, ((0, 32), (1, 4))),
        "out_weight": scatter_about(splits[6], (QUERY_HEADS * HEAD_DIMENSION, D), (QUERY_HEADS * HEAD_DIMENSION) ** -0.5, 0.0625, ((0, 4), (1, 32))),
        "block_lengths": uneven(splits[7], N_HST, N_HST * BLOCK_POSITIONS * 3 // 4, BLOCK_POSITIONS, 2).astype(jnp.int32),
    }


def attend_rows(query_rows, keys, values, allowed_fn):
    rows_all = query_rows.shape[0]
    step = min(512, rows_all)
    blocks = query_rows.reshape(rows_all // step, step, query_rows.shape[1], query_rows.shape[2])
    starts = jnp.arange(rows_all // step, dtype=jnp.int32) * step

    def one_block(items):
        block, start = items
        scores = jnp.einsum("rgd,sd->rgs", block.astype(jnp.float32), keys.astype(jnp.float32)) * (HEAD_DIMENSION ** -0.5)
        allowed = allowed_fn(start, step)
        scores = jnp.where(allowed[:, None, :], scores, -jnp.inf)
        top = jnp.max(scores, axis=-1)
        weights = jnp.exp(scores - top[..., None])
        total = jnp.sum(weights, axis=-1)
        probs = weights.astype(jnp.bfloat16)
        summed = jnp.einsum("rgs,sd->rgd", probs.astype(jnp.float32), values.astype(jnp.float32))
        return summed, top, total

    summed, top, total = lax.map(one_block, (blocks, starts))
    group_size = query_rows.shape[1]
    return (summed.reshape(rows_all, group_size, query_rows.shape[2]), top.reshape(rows_all, group_size), total.reshape(rows_all, group_size))


def reference(context_queries, context_keys, context_values, query_token_queries, query_token_keys, query_token_values, out_weight, block_lengths):
    group_size = QUERY_HEADS // KEY_VALUE_HEADS
    key_pos = jnp.arange(BLOCK_POSITIONS, dtype=jnp.int32)
    query_blocks = context_queries.reshape(N_HST, BLOCK_POSITIONS, KEY_VALUE_HEADS, group_size, HEAD_DIMENSION).transpose(0, 2, 1, 3, 4)
    key_blocks = context_keys.reshape(N_HST, BLOCK_POSITIONS, KEY_VALUE_HEADS, HEAD_DIMENSION).transpose(0, 2, 1, 3)
    value_blocks = context_values.reshape(N_HST, BLOCK_POSITIONS, KEY_VALUE_HEADS, HEAD_DIMENSION).transpose(0, 2, 1, 3)
    first_len = block_lengths[0]
    block_ids = jnp.arange(N_HST, dtype=jnp.int32)

    def block_one(items):
        q_here, k_here, v_here, index = items
        own_len = block_lengths[index]
        keys = jnp.concatenate([key_blocks[0], k_here], axis=1)
        values = jnp.concatenate([value_blocks[0], v_here], axis=1)

        def allowed(start, rows):
            rowpos = start + jnp.arange(rows, dtype=jnp.int32)
            anchor_ok = (key_pos < first_len) & (index > 0)
            local_ok = (key_pos[None, :] <= rowpos[:, None]) & (key_pos[None, :] < own_len)
            return jnp.concatenate([jnp.broadcast_to(anchor_ok[None, :], (rows, BLOCK_POSITIONS)), local_ok], axis=1)

        def head_one(parts):
            summed, top, total = attend_rows(parts[0], parts[1], parts[2], allowed)
            return (summed / total[..., None]).astype(jnp.bfloat16)

        result = lax.map(head_one, (q_here, keys, values))
        return result.transpose(1, 0, 2, 3).reshape(BLOCK_POSITIONS, QUERY_HEADS * HEAD_DIMENSION)

    context_out = lax.map(block_one, (query_blocks, key_blocks, value_blocks, block_ids)).reshape(CONTEXT_LENGTH, QUERY_HEADS * HEAD_DIMENSION)

    query_rows = query_token_queries.reshape(QUERY_LENGTH, KEY_VALUE_HEADS, group_size, HEAD_DIMENSION).transpose(1, 0, 2, 3)
    query_key_rows = query_token_keys.reshape(QUERY_LENGTH, KEY_VALUE_HEADS, HEAD_DIMENSION).transpose(1, 0, 2)
    query_value_rows = query_token_values.reshape(QUERY_LENGTH, KEY_VALUE_HEADS, HEAD_DIMENSION).transpose(1, 0, 2)
    query_pos = jnp.arange(QS, dtype=jnp.int32)

    def host_one(carry, items):
        k_here, v_here, index = items
        own_len = block_lengths[index]
        first = (index * QS).astype(jnp.int32)
        keys = jnp.concatenate([k_here, lax.dynamic_slice_in_dim(query_key_rows, first, QS, 1)], axis=1)
        values = jnp.concatenate([v_here, lax.dynamic_slice_in_dim(query_value_rows, first, QS, 1)], axis=1)

        def allowed(start, rows):
            rowpos = start + jnp.arange(rows, dtype=jnp.int32)
            block_ok = jnp.broadcast_to((key_pos < own_len)[None, :], (rows, BLOCK_POSITIONS))
            query_ok = (first + query_pos)[None, :] <= rowpos[:, None]
            return jnp.concatenate([block_ok, query_ok], axis=1)

        def head_two(parts):
            return attend_rows(parts[0], parts[1], parts[2], allowed)

        summed, top, total = lax.map(head_two, (query_rows, keys, values))
        total_o, best, total_l = carry
        new_best = jnp.maximum(best, top)
        old_scale = jnp.exp(best - new_best)
        scale = jnp.exp(top - new_best)
        carry = (total_o * old_scale[..., None] + summed * scale[..., None], new_best, total_l * old_scale + total * scale)
        return carry, None

    initial_state = (jnp.zeros((KEY_VALUE_HEADS, QUERY_LENGTH, group_size, HEAD_DIMENSION), jnp.float32), jnp.full((KEY_VALUE_HEADS, QUERY_LENGTH, group_size), -jnp.inf, jnp.float32), jnp.zeros((KEY_VALUE_HEADS, QUERY_LENGTH, group_size), jnp.float32))
    (total_o, best, total_l), unused = lax.scan(host_one, initial_state, (key_blocks, value_blocks, block_ids))
    attn = (total_o / total_l[..., None]).astype(jnp.bfloat16).transpose(1, 0, 2, 3).reshape(QUERY_LENGTH, QUERY_HEADS * HEAD_DIMENSION)
    query_out = jnp.dot(attn, out_weight, preferred_element_type=jnp.float32).astype(jnp.bfloat16)
    return context_out, query_out
```

```python
import functools
import math

import jax
import jax.numpy as jnp
from jax import lax
from jax.experimental import pallas as pl
from jax.experimental.pallas import tpu as pltpu
from jax.sharding import PartitionSpec as P

HEAD = 128
SCALE = math.log2(math.e) / math.sqrt(HEAD)
MASKED = -1e30
SAFE = 2.0**100
TILE = 512
STEP_HEADS = 4
NT = (((1,), (1,)), ((), ()))
LANES = 128
F32 = jnp.float32
BF16 = jnp.bfloat16

OWN, FIRST, Z, X, CORE, T, HOST = range(7)


def scores(keys, queries):
    return lax.dot_general(keys, queries, NT, preferred_element_type=F32)


def weigh(s, shift):
    return jnp.exp2((s - shift) * SCALE)


def mix(values_t, probs):
    return jnp.dot(values_t, probs.astype(BF16), preferred_element_type=F32)


def exact_update(s, values_t, state):
    top, total, acc = state
    new_top = jnp.maximum(top, jnp.max(s, axis=0, keepdims=True))
    probs, old = weigh(s, new_top), weigh(top, new_top)
    return (
        new_top,
        total * old + jnp.sum(probs, axis=0, keepdims=True),
        acc * old + mix(values_t, probs),
    )


def fresh(rows):
    return (
        jnp.full((1, rows), MASKED, F32),
        jnp.zeros((1, rows), F32),
        jnp.zeros((HEAD, rows), F32),
    )


def transposed(block):
    return block.astype(F32).T.astype(BF16)


def below(limit, start, count):
    key = start + lax.broadcasted_iota(jnp.int32, (count, limit.shape[1]), 0)
    return key <= limit


def local_kernel(tile, info, q, k, v, acc, stats, vt):
    keys = (tile + 1) * TILE
    half = TILE // 2

    @pl.when(pl.program_id(0) % 2 == 0)
    def _():
        vt[...] = transposed(v[...])

    own = info[OWN]
    row = tile * TILE + lax.broadcasted_iota(jnp.int32, (1, TILE), 1)
    limit = jnp.minimum(row, own - 1)
    wide = keys - half

    def score(h):
        query = q[:, h * HEAD : (h + 1) * HEAD]
        s = scores(k[0:wide, :], query)
        late = scores(k[wide:keys, :], query[half:, :])
        return s, late

    pending = score(0)
    for h in range(STEP_HEADS):
        s, late = pending
        if h + 1 < STEP_HEADS:
            pending = score(h + 1)
        shift = s[0:1, :]
        p = weigh(jnp.where(below(limit, 0, wide), s, MASKED), shift)
        pl_ = weigh(
            jnp.where(below(limit[:, half:], wide, half), late, MASKED), shift[:, half:]
        )
        total = jnp.sum(p, axis=0, keepdims=True)
        total_late = jnp.sum(pl_, axis=0, keepdims=True)
        stats[0, h : h + 1, 0:half] = total[:, :half]
        stats[0, h : h + 1, half:] = total[:, half:] + total_late
        stats[0, STEP_HEADS + h : STEP_HEADS + h + 1, :] = shift
        o = mix(vt[:, 0:wide], p)
        o_late = mix(vt[:, wide:keys], pl_)
        acc[0, h, :, 0:half] = o[:, :half]
        acc[0, h, :, half:] = o[:, half:] + o_late

    @pl.when(jnp.logical_not(jnp.max(stats[0, 0:STEP_HEADS, :]) < SAFE))
    def _():
        for h in range(STEP_HEADS):
            query = q[:, h * HEAD : (h + 1) * HEAD]

            def chunk(j, state):
                at = pl.multiple_of(j * half, half)
                s = scores(k[pl.ds(at, half), :], query)
                s = jnp.where(below(limit, at, half), s, MASKED)
                return exact_update(s, vt[:, pl.ds(at, half)], state)

            top, total, o = lax.fori_loop(0, keys // half, chunk, fresh(TILE))
            stats[0, h : h + 1, :] = total
            stats[0, STEP_HEADS + h : STEP_HEADS + h + 1, :] = top
            acc[0, h] = o


def local_part(tile, info, q, k, v):
    keys = (tile + 1) * TILE
    steps = q.shape[1] // (STEP_HEADS * HEAD)
    return pl.pallas_call(
        functools.partial(local_kernel, tile),
        grid_spec=pltpu.PrefetchScalarGridSpec(
            num_scalar_prefetch=1,
            grid=(steps,),
            in_specs=[
                pl.BlockSpec((TILE, STEP_HEADS * HEAD), lambda s, _: (tile, s)),
                pl.BlockSpec((keys, HEAD), lambda s, _: (0, s // 2)),
                pl.BlockSpec((keys, HEAD), lambda s, _: (0, s // 2)),
            ],
            out_specs=[
                pl.BlockSpec((1, STEP_HEADS, HEAD, TILE), lambda s, _: (s, 0, 0, 0)),
                pl.BlockSpec((1, 2 * STEP_HEADS, TILE), lambda s, _: (s, 0, 0)),
            ],
            scratch_shapes=[pltpu.VMEM((HEAD, keys), BF16)],
        ),
        out_shape=[
            jax.ShapeDtypeStruct((steps, STEP_HEADS, HEAD, TILE), F32),
            jax.ShapeDtypeStruct((steps, 2 * STEP_HEADS, TILE), F32),
        ],
        compiler_params=pltpu.CompilerParams(vmem_limit_bytes=48 << 20),
        name=f"local_{tile}",
    )(info, q, k, v)


def anchor_kernel(first_step, info, q, p0, p1, p2, p3, acc_in, stats_in, *rest):
    out, kk, vt, acc, stats = rest[-5:]
    quarter = p0.shape[0] // 2
    step = first_step + pl.program_id(0)

    @pl.when((pl.program_id(0) == 0) | (step % 2 == 0))
    def _():
        for back, piece in enumerate((p0, p1, p2, p3)):
            at = pl.multiple_of(((info[X] + 4 - back) & 3) * quarter, quarter)
            kk[pl.ds(at, quarter), :] = piece[0:quarter, :]
            vt[:, pl.ds(at, quarter)] = transposed(piece[quarter:, :])

    n = info[FIRST]

    def start():
        stats[...] = stats_in[0]
        acc[...] = acc_in[0]

    def add(at, count, masked):
        def score(h):
            return scores(kk[pl.ds(at, count), :], q[:, h * HEAD : (h + 1) * HEAD])

        limit = jnp.full((1, TILE), n - 1, jnp.int32)
        pending = score(0)
        for h in range(STEP_HEADS):
            s = pending
            if h + 1 < STEP_HEADS:
                pending = score(h + 1)
            if masked:
                s = jnp.where(below(limit, at, count), s, MASKED)
            p = weigh(s, stats[STEP_HEADS + h : STEP_HEADS + h + 1, :])
            stats[h : h + 1, :] += jnp.sum(p, axis=0, keepdims=True)
            acc[h] += mix(vt[:, pl.ds(at, count)], p)

    start()
    wide = 2 * quarter
    full = n // wide
    left = n - full * wide

    @pl.loop(0, full)
    def _(j):
        add(pl.multiple_of(j * wide, wide), wide, False)

    tail = pl.multiple_of(full * wide, wide)

    @pl.when(left > quarter)
    def _():
        add(tail, wide, True)

    @pl.when((left > 0) & (left <= quarter))
    def _():
        add(tail, quarter, True)

    @pl.when(jnp.logical_not(jnp.max(stats[0:STEP_HEADS, :]) < SAFE))
    def _():
        start()
        limit = jnp.full((1, TILE), n - 1, jnp.int32)
        for h in range(STEP_HEADS):
            query = q[:, h * HEAD : (h + 1) * HEAD]

            def chunk(j, state):
                at = pl.multiple_of(j * quarter, quarter)
                s = scores(kk[pl.ds(at, quarter), :], query)
                s = jnp.where(below(limit, at, quarter), s, MASKED)
                return exact_update(s, vt[:, pl.ds(at, quarter)], state)

            begin = (stats[STEP_HEADS + h : STEP_HEADS + h + 1, :], stats[h : h + 1, :], acc[h])
            top, total, o = lax.fori_loop(0, (n + quarter - 1) // quarter, chunk, begin)
            stats[h : h + 1, :] = total
            acc[h] = o

    for h in range(STEP_HEADS):
        o = acc[h] / stats[h : h + 1, :]
        out[:, h * HEAD : (h + 1) * HEAD] = o.T.astype(BF16)


def anchor_part(tile, group, info, q, pieces, acc, stats, out):
    wide = STEP_HEADS * HEAD
    first = group * 2
    rows = pieces[0].shape[0]
    in_specs = [pl.BlockSpec((TILE, wide), lambda s, _: (tile, first + s))]
    in_specs += [pl.BlockSpec((rows, HEAD), lambda s, _: (0, (first + s) // 2))] * 4
    in_specs += [
        pl.BlockSpec((1, STEP_HEADS, HEAD, TILE), lambda s, _: (first + s, 0, 0, 0)),
        pl.BlockSpec((1, 2 * STEP_HEADS, TILE), lambda s, _: (first + s, 0, 0)),
    ]
    args = [info, q, *pieces, acc, stats]
    aliases = {}
    if out is not None:
        in_specs.append(pl.BlockSpec(memory_space=pl.ANY))
        aliases = {len(args): 0}
        args.append(out)
    return pl.pallas_call(
        functools.partial(anchor_kernel, first),
        grid_spec=pltpu.PrefetchScalarGridSpec(
            num_scalar_prefetch=1,
            grid=(2,),
            in_specs=in_specs,
            out_specs=pl.BlockSpec((TILE, wide), lambda s, _: (tile, first + s)),
            scratch_shapes=[
                pltpu.VMEM((2 * rows, HEAD), BF16),
                pltpu.VMEM((HEAD, 2 * rows), BF16),
                pltpu.VMEM((STEP_HEADS, HEAD, TILE), F32),
                pltpu.VMEM((2 * STEP_HEADS, TILE), F32),
            ],
        ),
        out_shape=jax.ShapeDtypeStruct(q.shape, BF16),
        input_output_aliases=aliases,
        compiler_params=pltpu.CompilerParams(vmem_limit_bytes=48 << 20),
        name=f"anchor_{tile}_{group}",
    )(*args)


def split3(value):
    hi = value.astype(BF16).astype(F32)
    mid = (value - hi).astype(BF16).astype(F32)
    return hi, mid, value - hi - mid


def query_kernel(info, *refs):
    pieces, (k, v, kq, vq, near, far, vt, vtq, lse, totals, tops, accs) = refs[:8], refs[8:]
    step = pl.program_id(0)
    rows = 8 * pieces[0].shape[0]
    wide = 2 * rows
    keys = k.shape[0]
    share = kq.shape[0]

    @pl.when(step % 2 == 0)
    def _():
        vt[...] = transposed(v[...])
        vtq[...] = jnp.concatenate(
            [vq[...].astype(F32), jnp.zeros((LANES - share, HEAD), F32)], axis=0
        ).T.astype(BF16)

    own = info[OWN]
    lane = lax.broadcasted_iota(jnp.int32, (1, wide), 1)
    home_x = (info[X] + 4 - ((lane >> 3) & 3)) & 3
    home_z = (info[Z] + 4 - ((lane >> 5) & 3)) & 3
    home_core = (info[CORE] + ((lane >> 7) & 1)) & 1
    row = ((home_z * 4 + home_x) * 2 + home_core) * share + (lane & 7)
    limit = jnp.full((1, wide), own - 1, jnp.int32)
    late_limit = jnp.minimum(row - info[HOST] * share, share - 1)
    query_keys = jnp.concatenate(
        [kq[...].astype(F32), jnp.zeros((16 - share, HEAD), F32)], axis=0
    ).astype(BF16)

    def pair(a):
        parts = [
            piece[:, h * HEAD : (h + 1) * HEAD] for h in (2 * a, 2 * a + 1) for piece in pieces
        ]
        return jnp.concatenate(parts, axis=0)

    def late_score(query):
        return jnp.where(below(late_limit, 0, 16), scores(query_keys, query), MASKED)

    def score(a):
        query = pair(a)
        return scores(k[...], query), late_score(query)

    pending = score(0)
    for a in range(STEP_HEADS // 2):
        s, late = pending
        if a + 1 < STEP_HEADS // 2:
            pending = score(a + 1)
        shift = s[0:1, :]
        p = weigh(jnp.where(below(limit, 0, keys), s, MASKED), shift)
        pq = weigh(late, shift)
        totals[a : a + 1, :] = jnp.sum(p, axis=0, keepdims=True) + jnp.sum(
            pq, axis=0, keepdims=True
        )
        tops[a : a + 1, :] = shift
        accs[a] = mix(vt[...], p) + mix(vtq[:, 0:16], pq)

    @pl.when(jnp.logical_not(jnp.max(totals[0 : STEP_HEADS // 2, :]) < SAFE))
    def _():
        part = keys // 4
        for a in range(STEP_HEADS // 2):
            query = pair(a)

            def chunk(j, state):
                at = pl.multiple_of(j * part, part)
                s = scores(k[pl.ds(at, part), :], query)
                s = jnp.where(below(limit, at, part), s, MASKED)
                return exact_update(s, vt[:, pl.ds(at, part)], state)

            state = lax.fori_loop(0, 4, chunk, fresh(wide))
            top, total, o = exact_update(late_score(query), vtq[:, 0:16], state)
            totals[a : a + 1, :] = total
            tops[a : a + 1, :] = top
            accs[a] = o

    half = rows // 2
    for a in range(STEP_HEADS // 2):
        total = totals[a : a + 1, :]
        o = accs[a] / total
        log_total = tops[a : a + 1, :] * SCALE + jnp.log(total) * math.log2(math.e)
        for b in range(2):
            h = 2 * a + b
            lse[pl.ds(step * STEP_HEADS + h, 1), :] = log_total[:, b * rows : (b + 1) * rows]
            at = pl.multiple_of((step * STEP_HEADS + h) * HEAD, HEAD)
            o_rows = o[:, b * rows : (b + 1) * rows].T.astype(BF16)
            near[:, pl.ds(at, HEAD)] = o_rows[:half, :]
            far[:, pl.ds(at, HEAD)] = o_rows[half:, :]

    @pl.when(step == pl.num_programs(0) - 1)
    def _():
        heads = lse.shape[0]
        parts = split3(lse[...])
        columns = jnp.concatenate(
            [*parts, jnp.zeros((LANES - 3 * heads, rows), F32)], axis=0
        ).T.astype(BF16)
        at = heads * HEAD
        near[:, at : at + LANES] = columns[:half, :]
        far[:, at : at + LANES] = columns[half:, :]


def query_part(info, pieces, k, v, kq, vq):
    rows, width = pieces[0].shape
    steps = width // (STEP_HEADS * HEAD)
    keys = k.shape[0]
    share = kq.shape[0]
    half = jax.ShapeDtypeStruct((4 * rows, width + LANES), BF16)
    return pl.pallas_call(
        query_kernel,
        grid_spec=pltpu.PrefetchScalarGridSpec(
            num_scalar_prefetch=1,
            grid=(steps,),
            in_specs=[pl.BlockSpec((rows, STEP_HEADS * HEAD), lambda s, _: (0, s))] * 8
            + [pl.BlockSpec((keys, HEAD), lambda s, _: (0, s // 2))] * 2
            + [pl.BlockSpec((share, HEAD), lambda s, _: (0, s // 2))] * 2,
            out_specs=[pl.BlockSpec(half.shape, lambda s, _: (0, 0))] * 2,
            scratch_shapes=[
                pltpu.VMEM((HEAD, keys), BF16),
                pltpu.VMEM((HEAD, LANES), BF16),
                pltpu.VMEM((width // HEAD, 8 * rows), F32),
                pltpu.VMEM((8, 16 * rows), F32),
                pltpu.VMEM((8, 16 * rows), F32),
                pltpu.VMEM((STEP_HEADS // 2, HEAD, 16 * rows), F32),
            ],
        ),
        out_shape=[half, half],
        compiler_params=pltpu.CompilerParams(vmem_limit_bytes=48 << 20),
        name="query_part",
    )(info, *pieces, k, v, kq, vq)


def merge_kernel(count, roll, last, *refs):
    parts, outs = refs[:count], refs[count:]
    rows = parts[0].shape[0]
    heads = parts[0].shape[1] // HEAD - 1
    at = heads * HEAD
    lane = lax.broadcasted_iota(jnp.int32, (rows, LANES), 1)
    source = lax.broadcasted_iota(jnp.int32, (LANES, LANES), 0)
    columns = jnp.zeros((rows, LANES), F32)
    each = rows // len(outs)
    block = rows // 4

    def turned(value, back):
        if not roll or back == 0:
            return value
        cut = rows - back * block
        return jnp.concatenate([value[cut:, :], value[:cut, :]], axis=0)

    logs = [part[:, at : at + LANES] for part in parts]
    for h in range(heads):
        pick = ((source == h) | (source == heads + h) | (source == 2 * heads + h)).astype(F32)
        pick = pick.astype(BF16)
        log = [
            turned(jnp.dot(c, pick, preferred_element_type=F32), i) for i, c in enumerate(logs)
        ]
        top = functools.reduce(jnp.maximum, log)
        weights = [jnp.exp2(value - top) for value in log]
        total = functools.reduce(jnp.add, weights)
        merged = functools.reduce(
            jnp.add,
            [
                w * turned(part[:, h * HEAD : (h + 1) * HEAD].astype(F32), i)
                for i, (w, part) in enumerate(zip(weights, parts))
            ],
        )
        merged = (merged / total).astype(BF16)
        for i, out in enumerate(outs):
            out[:, h * HEAD : (h + 1) * HEAD] = merged[i * each : (i + 1) * each, :]
        if not last:
            hi, mid, lo = split3(top + jnp.log(total) * math.log2(math.e))
            columns = jnp.where(lane == h, hi, columns)
            columns = jnp.where(lane == heads + h, mid, columns)
            columns = jnp.where(lane == 2 * heads + h, lo, columns)
    if not last:
        for i, out in enumerate(outs):
            out[:, at : at + LANES] = columns[i * each : (i + 1) * each, :].astype(BF16)


def merge(parts, outs, roll=False, last=False, name="merge"):
    rows, width = parts[0].shape
    shape = jax.ShapeDtypeStruct((rows // outs, width - LANES if last else width), BF16)
    whole = pl.BlockSpec(memory_space=pltpu.VMEM)
    return pl.pallas_call(
        functools.partial(merge_kernel, len(parts), roll, last),
        in_specs=[whole] * len(parts),
        out_specs=[whole] * outs,
        out_shape=[shape] * outs,
        compiler_params=pltpu.CompilerParams(vmem_limit_bytes=32 << 20),
        name=name,
    )(*parts)


def project_kernel(info, *refs):
    pieces, w, outs, whole = refs[:8], refs[8], refs[9:13], refs[13]
    rows = pieces[0].shape[0]
    attn = jnp.concatenate([piece[...] for piece in pieces], axis=0)
    product = jnp.dot(attn, w[...], preferred_element_type=F32)
    block = rows // 4
    for i in range(8):
        home_core = (info[CORE] + i // 4) & 1
        home_z = (info[Z] + 4 - i % 4) & 3
        for j in range(4):
            home_x = (info[X] + 4 - j) & 3
            at = pl.multiple_of(((home_z * 4 + home_x) * 2 + home_core) * block, block)
            start = i * rows + j * block
            whole[pl.ds(at, block), :] = product[start : start + block, :]
    each = outs[0].shape[0]
    for ahead, out in enumerate(outs):
        at = pl.multiple_of(((info[T] + ahead) & 3) * each, each)
        out[...] = whole[pl.ds(at, each), :]


def project(info, pieces, w):
    rows = 8 * pieces[0].shape[0]
    whole = pl.BlockSpec(memory_space=pltpu.VMEM)
    return pl.pallas_call(
        project_kernel,
        grid_spec=pltpu.PrefetchScalarGridSpec(
            num_scalar_prefetch=1,
            grid=(),
            in_specs=[whole] * 9,
            out_specs=[whole] * 4,
            scratch_shapes=[pltpu.VMEM((rows, w.shape[1]), F32)],
        ),
        out_shape=[jax.ShapeDtypeStruct((rows // 4, w.shape[1]), F32)] * 4,
        compiler_params=pltpu.CompilerParams(vmem_limit_bytes=32 << 20),
        name="project",
    )(info, *pieces, w)


def host_at(z, x, core):
    return ((z % 4) * 4 + x % 4) * 2 + core


def moved(dz, dx, swap=0, cores=(0, 1)):
    return [
        (host_at(z, x, c), host_at(z + dz, x + dx, c ^ swap))
        for z in range(4)
        for x in range(4)
        for c in cores
    ]


def send(value, perm):
    return lax.ppermute(value, "hst", perm)


def after(value, *others):
    return lax.optimization_barrier((value, *others))[0]


def shards(cq, ck, cv, qq, qk, qv, w, lengths):
    host = lax.axis_index("hst")
    z, x, core = host // 8, (host // 2) % 4, host % 2
    own = jnp.sum(jnp.where(jnp.arange(lengths.shape[0], dtype=jnp.int32) == host, lengths, 0))
    first = jnp.where(host > 0, lengths[0], 0)
    info = jnp.stack([own, first, z, x, core, lax.axis_index("tensor"), host]).astype(jnp.int32)

    by_x = [qq] + [send(qq, moved(0, d)) for d in (1, 3, 2)]
    by_x = [by_x[0], by_x[1], by_x[3], by_x[2]]
    tile1 = local_part(1, info, cq, ck, cv)
    row_q = jnp.concatenate(by_x, axis=0)
    row_q = after(row_q, tile1[1])
    by_z = [send(row_q, moved(d, 0)) for d in (1, 3, 2)]
    by_z = [row_q, by_z[0], by_z[2], by_z[1]]

    quarter = ck.shape[0] // 4
    kv = [
        jnp.concatenate([ck[i * quarter : (i + 1) * quarter], cv[i * quarter : (i + 1) * quarter]])
        for i in range(4)
    ]
    kv = [after(piece, row_q) for piece in kv]
    got = kv[0]
    for d in (1, 3, 2):
        got = jnp.where(x == d, send(kv[d], [(0, host_at(0, d, 0))]), got)

    tile0 = local_part(0, after(info, row_q), cq, ck, cv)
    by_z = [after(piece, tile0[1]) for piece in by_z]
    pieces = by_z + [send(piece, moved(0, 0, 1)) for piece in by_z]

    down = after(got, by_z[1])
    mine = down
    for d in (1, 3, 2):
        mine = jnp.where(
            z == d, send(down, [(host_at(0, i, 0), host_at(d, i, 0)) for i in range(4)]), mine
        )

    near, far = query_part(info, pieces, ck, cv, qk, qv)
    other = send(far, moved(0, 0, 1))
    mine = after(mine, near)
    along = [mine] + [send(mine, moved(0, d, 0, (0,))) for d in (1, 2, 3)]
    dz = merge([near, other], 4, name="merge_core")
    from_z = [send(dz[d], moved(-d, 0)) for d in (1, 3, 2)]
    crossed = [send(piece, [(h, h + 1) for h in range(0, 32, 2)]) for piece in along]
    anchor = [jnp.where(core == 0, a, b) for a, b in zip(along, crossed)]
    (mine_q,) = merge([dz[0], *from_z], 1, name="merge_z")
    from_x = [send(mine_q, moved(0, d)) for d in (1, 2, 3)]
    out = anchor_part(1, 0, after(info, mine_q), cq, anchor, *tile1, None)
    (attn,) = merge([mine_q, *(after(p, out) for p in from_x)], 1, True, True, name="merge_x")
    others = [send(attn, moved(d, 0)) for d in (1, 2, 3)]
    out = anchor_part(1, 1, after(info, attn), cq, anchor, *tile1, out)
    attn_z = [attn] + [after(p, out) for p in others]
    attn_all = attn_z + [send(piece, moved(0, 0, 1)) for piece in attn_z]
    sums = project(info, attn_all, w)
    swaps = [
        lax.ppermute(sums[d], "tensor", [(i, (i + d) % 4) for i in range(4)]) for d in (1, 2, 3)
    ]
    last_info = after(info, sums[0])
    out = anchor_part(0, 0, last_info, cq, anchor, *tile0, out)
    out = anchor_part(0, 1, last_info, cq, anchor, *tile0, out)
    query_out = (sums[0] + swaps[0] + swaps[1] + swaps[2]).astype(BF16)
    return out, query_out


def solution(mesh):
    in_specs = (
        P("hst", "tensor"),
        P("hst", "tensor"),
        P("hst", "tensor"),
        P("hst", "tensor"),
        P("hst", "tensor"),
        P("hst", "tensor"),
        P("tensor", "hst"),
        P(),
    )
    out_specs = (P("hst", "tensor"), P("tensor", "hst"))
    return jax.shard_map(shards, mesh=mesh, in_specs=in_specs, out_specs=out_specs, check_vma=False)
```

```python
import functools
import math

import jax
import jax.numpy as jnp
from jax import lax
from jax.experimental import pallas as pl
from jax.experimental.pallas import tpu as pltpu
from jax.sharding import PartitionSpec as P

HEAD = 128
SCALE = math.log2(math.e) / math.sqrt(HEAD)
MASKED = -1e30
SAFE = 2.0**100
TILE = 512
STEP_HEADS = 4
NT = (((1,), (1,)), ((), ()))
LANES = 128
F32 = jnp.float32
BF16 = jnp.bfloat16

QUARTER = 256
BIG = 60 << 20
MIDDLE = 32 << 20


def place():
    host = lax.axis_index("hst")
    return host, host >> 3, (host >> 1) & 3, host & 1


def scores(keys, queries):
    return lax.dot_general(keys, queries, NT, preferred_element_type=F32)


def weigh(s, shift):
    return jnp.exp2((s - shift) * SCALE)


def mix(values_t, probs):
    return jnp.dot(values_t, probs.astype(BF16), preferred_element_type=F32)


def exact_update(s, values_t, state):
    top, total, acc = state
    new_top = jnp.maximum(top, jnp.max(s, axis=0, keepdims=True))
    probs, old = weigh(s, new_top), weigh(top, new_top)
    return (
        new_top,
        total * old + jnp.sum(probs, axis=0, keepdims=True),
        acc * old + mix(values_t, probs),
    )


def fresh(rows):
    return (
        jnp.full((1, rows), MASKED, F32),
        jnp.zeros((1, rows), F32),
        jnp.zeros((HEAD, rows), F32),
    )


def below(limit, start, count):
    key = start + lax.broadcasted_iota(jnp.int32, (count, limit.shape[1]), 0)
    return key <= limit


def turn_kernel(v, out):
    for j in range(out.shape[0]):
        out[j] = v[j * QUARTER : (j + 1) * QUARTER, :].astype(F32).T.astype(BF16)


def turn(v):
    quarters = v.shape[0] // QUARTER
    whole = pl.BlockSpec(memory_space=pltpu.VMEM)
    return pl.pallas_call(
        turn_kernel,
        in_specs=[whole],
        out_specs=whole,
        out_shape=jax.ShapeDtypeStruct((quarters, v.shape[1], QUARTER), BF16),
        compiler_params=pltpu.CompilerParams(vmem_limit_bytes=16 << 20),
        name="turn",
    )(v)


def beside(vt, first, count):
    parts = [vt[j, :, :] for j in range(first, first + count)]
    return parts[0] if count == 1 else jnp.concatenate(parts, axis=1)


def local_kernel(tile, lengths, q, k, vt, acc, stats):
    keys = (tile + 1) * TILE
    half = QUARTER
    heads = q.shape[1] // HEAD
    own = lengths[place()[0]]
    row = tile * TILE + lax.broadcasted_iota(jnp.int32, (1, TILE), 1)
    limit = jnp.minimum(row, own - 1)
    wide = keys - half

    def score(h):
        query = q[:, h * HEAD : (h + 1) * HEAD]
        s = scores(k[0:wide, :], query)
        late = scores(k[wide:keys, :], query[half:, :])
        return s, late

    pending = score(0)
    for h in range(heads):
        s, late = pending
        if h + 1 < heads:
            pending = score(h + 1)
        shift = s[0:1, :]
        p = weigh(jnp.where(below(limit, 0, wide), s, MASKED), shift)
        p_late = weigh(
            jnp.where(below(limit[:, half:], wide, half), late, MASKED), shift[:, half:]
        )
        total = jnp.sum(p, axis=0, keepdims=True)
        total_late = jnp.sum(p_late, axis=0, keepdims=True)
        stats[0, h : h + 1, 0:half] = total[:, :half]
        stats[0, h : h + 1, half:] = total[:, half:] + total_late
        stats[0, STEP_HEADS + h : STEP_HEADS + h + 1, :] = shift
        o = mix(beside(vt, 0, wide // half), p)
        o_late = mix(vt[wide // half, :, :], p_late)
        acc[0, h, :, 0:half] = o[:, :half]
        acc[0, h, :, half:] = o[:, half:] + o_late

    @pl.when(jnp.logical_not(jnp.max(stats[0, 0:STEP_HEADS, :]) < SAFE))
    def _():
        for h in range(heads):
            query = q[:, h * HEAD : (h + 1) * HEAD]

            def chunk(j, state):
                at = pl.multiple_of(j * half, half)
                s = scores(k[pl.ds(at, half), :], query)
                s = jnp.where(below(limit, at, half), s, MASKED)
                return exact_update(s, vt[j], state)

            top, total, o = lax.fori_loop(0, keys // half, chunk, fresh(TILE))
            stats[0, h : h + 1, :] = total
            stats[0, STEP_HEADS + h : STEP_HEADS + h + 1, :] = top
            acc[0, h] = o


def local_part(tile, lengths, q, k, vt):
    keys = (tile + 1) * TILE
    heads = STEP_HEADS
    steps = q.shape[1] // (heads * HEAD)
    return pl.pallas_call(
        functools.partial(local_kernel, tile),
        grid_spec=pltpu.PrefetchScalarGridSpec(
            num_scalar_prefetch=1,
            grid=(steps,),
            in_specs=[
                pl.BlockSpec((TILE, heads * HEAD), lambda g, _: (tile, g)),
                pl.BlockSpec((keys, HEAD), lambda g, _: (0, g // 2)),
                pl.BlockSpec((keys // QUARTER, HEAD, QUARTER), lambda g, _: (0, g // 2, 0)),
            ],
            out_specs=[
                pl.BlockSpec((1, STEP_HEADS, HEAD, TILE), lambda g, _: (g, 0, 0, 0)),
                pl.BlockSpec((1, 2 * STEP_HEADS, TILE), lambda g, _: (g, 0, 0)),
            ],
        ),
        out_shape=[
            jax.ShapeDtypeStruct((steps, STEP_HEADS, HEAD, TILE), F32),
            jax.ShapeDtypeStruct((steps, 2 * STEP_HEADS, TILE), F32),
        ],
        compiler_params=pltpu.CompilerParams(vmem_limit_bytes=BIG),
        name=f"local_{tile}",
    )(lengths, q, k, vt)


def anchor_kernel(lengths, q, k, vt, acc, stats, *rest):
    out, totals = rest[-2:]
    n = jnp.where(place()[0] > 0, lengths[0], 0)
    quarters = (n + QUARTER - 1) // QUARTER
    limit = jnp.full((1, TILE), n - 1, jnp.int32)

    def finish(h, o, total):
        out[:, h * HEAD : (h + 1) * HEAD] = (o * (1.0 / total)).T.astype(BF16)

    def query(h):
        return q[:, h * HEAD : (h + 1) * HEAD]

    @pl.when(quarters == 0)
    def _():
        totals[...] = stats[0, 0:STEP_HEADS, :]
        for h in range(STEP_HEADS):
            finish(h, acc[0, h], stats[0, h : h + 1, :])

    def run(count):
        near = (count - 1) * QUARTER

        def score(h):
            late = scores(k[near : near + QUARTER, :], query(h))
            return late if near == 0 else (scores(k[0:near, :], query(h)), late)

        pending = score(0)
        for h in range(STEP_HEADS):
            s = pending
            if h + 1 < STEP_HEADS:
                pending = score(h + 1)
            shift = stats[0, STEP_HEADS + h : STEP_HEADS + h + 1, :]
            late = s if near == 0 else s[1]
            p = weigh(jnp.where(below(limit, near, QUARTER), late, MASKED), shift)
            total = stats[0, h : h + 1, :] + jnp.sum(p, axis=0, keepdims=True)
            p = p.astype(BF16)
            if near:
                p_near = weigh(s[0], shift)
                total = total + jnp.sum(p_near, axis=0, keepdims=True)
                p = jnp.concatenate([p_near.astype(BF16), p], axis=0)
            totals[h : h + 1, :] = total
            finish(h, acc[0, h] + mix(beside(vt, 0, count), p), total)

    for count in range(1, vt.shape[0] + 1):
        pl.when(quarters == count)(functools.partial(run, count))

    @pl.when(jnp.logical_not(jnp.max(totals[...]) < SAFE))
    def _():
        for h in range(STEP_HEADS):

            def chunk(j, state):
                at = pl.multiple_of(j * QUARTER, QUARTER)
                s = scores(k[pl.ds(at, QUARTER), :], query(h))
                s = jnp.where(below(limit, at, QUARTER), s, MASKED)
                return exact_update(s, vt[j], state)

            begin = (
                stats[0, STEP_HEADS + h : STEP_HEADS + h + 1, :],
                stats[0, h : h + 1, :],
                acc[0, h],
            )
            top, total, o = lax.fori_loop(0, quarters, chunk, begin)
            finish(h, o, total)


def anchor_part(tile, first, steps, lengths, q, k, vt, acc, stats, out):
    wide = STEP_HEADS * HEAD
    in_specs = [
        pl.BlockSpec((TILE, wide), lambda s, _: (tile, first + s)),
        pl.BlockSpec((k.shape[0], HEAD), lambda s, _: (0, (first + s) // 2)),
        pl.BlockSpec((vt.shape[0], HEAD, QUARTER), lambda s, _: (0, (first + s) // 2, 0)),
        pl.BlockSpec((1, STEP_HEADS, HEAD, TILE), lambda s, _: (first + s, 0, 0, 0)),
        pl.BlockSpec((1, 2 * STEP_HEADS, TILE), lambda s, _: (first + s, 0, 0)),
    ]
    args = [lengths, q, k, vt, acc, stats]
    aliases = {}
    if out is not None:
        in_specs.append(pl.BlockSpec(memory_space=pl.ANY))
        aliases = {len(args): 0}
        args.append(out)
    return pl.pallas_call(
        anchor_kernel,
        grid_spec=pltpu.PrefetchScalarGridSpec(
            num_scalar_prefetch=1,
            grid=(steps,),
            in_specs=in_specs,
            out_specs=pl.BlockSpec((TILE, wide), lambda s, _: (tile, first + s)),
            scratch_shapes=[pltpu.VMEM((STEP_HEADS, TILE), F32)],
        ),
        out_shape=jax.ShapeDtypeStruct(q.shape, BF16),
        input_output_aliases=aliases,
        compiler_params=pltpu.CompilerParams(vmem_limit_bytes=BIG),
        name=f"anchor_{tile}_{first}",
    )(*args)


def split3(value):
    hi = value.astype(BF16).astype(F32)
    mid = (value - hi).astype(BF16).astype(F32)
    return hi, mid, value - hi - mid


def query_kernel(lengths, *refs):
    pieces, (k, vt, kq, vq, near, far, lse, totals) = refs[:8], refs[8:]
    step = pl.program_id(0)
    rows = 8 * pieces[0].shape[0]
    half = rows // 2
    wide = 2 * rows
    keys = k.shape[0]
    share = kq.shape[0]
    host, z, x, core = place()
    lane = lax.broadcasted_iota(jnp.int32, (1, wide), 1)
    home_x = (x + 4 - ((lane >> 3) & 3)) & 3
    home_z = (z + 4 - ((lane >> 5) & 3)) & 3
    home_core = (core + ((lane >> 7) & 1)) & 1
    row = ((home_z * 4 + home_x) * 2 + home_core) * share + (lane & 7)
    limit = jnp.full((1, wide), lengths[host] - 1, jnp.int32)
    late_limit = jnp.minimum(row - host * share, share - 1)
    query_keys = jnp.concatenate(
        [kq[...].astype(F32), jnp.zeros((16 - share, HEAD), F32)], axis=0
    ).astype(BF16)
    query_values = jnp.concatenate(
        [vq[...].astype(F32), jnp.zeros((LANES - share, HEAD), F32)], axis=0
    ).T[:, 0:16].astype(BF16)

    def pair(a):
        parts = [piece[:, h * HEAD : (h + 1) * HEAD] for h in (2 * a, 2 * a + 1) for piece in pieces]
        return jnp.concatenate(parts, axis=0)

    def late_score(query):
        return jnp.where(below(late_limit, 0, 16), scores(query_keys, query), MASKED)

    def score(a):
        query = pair(a)
        return scores(k[...], query), late_score(query)

    def finish(a, o, total, top):
        totals[a : a + 1, :] = total
        o = o * (1.0 / total)
        log_total = top * SCALE + jnp.log(total) * math.log2(math.e)
        for b in range(2):
            h = step * STEP_HEADS + 2 * a + b
            lse[pl.ds(h, 1), :] = log_total[:, b * rows : (b + 1) * rows]
            at = pl.multiple_of(h * HEAD, HEAD)
            o_rows = o[:, b * rows : (b + 1) * rows].T
            near[:, pl.ds(at, HEAD)] = o_rows[:half, :]
            far[:, pl.ds(at, HEAD)] = o_rows[half:, :]

    values = beside(vt, 0, keys // QUARTER)
    pending = score(0)
    for a in range(STEP_HEADS // 2):
        s, late = pending
        if a + 1 < STEP_HEADS // 2:
            pending = score(a + 1)
        shift = s[0:1, :]
        p = weigh(jnp.where(below(limit, 0, keys), s, MASKED), shift)
        p_late = weigh(late, shift)
        total = jnp.sum(p, axis=0, keepdims=True) + jnp.sum(p_late, axis=0, keepdims=True)
        finish(a, mix(values, p) + mix(query_values, p_late), total, shift)

    @pl.when(jnp.logical_not(jnp.max(totals[...]) < SAFE))
    def _():
        for a in range(STEP_HEADS // 2):
            query = pair(a)

            def chunk(j, state):
                at = pl.multiple_of(j * QUARTER, QUARTER)
                s = scores(k[pl.ds(at, QUARTER), :], query)
                s = jnp.where(below(limit, at, QUARTER), s, MASKED)
                return exact_update(s, vt[j], state)

            state = lax.fori_loop(0, keys // QUARTER, chunk, fresh(wide))
            top, total, o = exact_update(late_score(query), query_values, state)
            finish(a, o, total, top)

    @pl.when(step == pl.num_programs(0) - 1)
    def _():
        count = lse.shape[0]
        parts = split3(lse[...])
        columns = jnp.concatenate(
            [*parts, jnp.zeros((LANES - 3 * count, rows), F32)], axis=0
        ).T
        at = count * HEAD
        near[:, at : at + LANES] = columns[:half, :]
        far[:, at : at + LANES] = columns[half:, :]


def query_part(lengths, pieces, k, vt, kq, vq):
    rows, width = pieces[0].shape
    keys = k.shape[0]
    share = kq.shape[0]
    half = jax.ShapeDtypeStruct((4 * rows, width + LANES), F32)
    return pl.pallas_call(
        query_kernel,
        grid_spec=pltpu.PrefetchScalarGridSpec(
            num_scalar_prefetch=1,
            grid=(width // (STEP_HEADS * HEAD),),
            in_specs=[pl.BlockSpec((rows, STEP_HEADS * HEAD), lambda g, _: (0, g))] * 8
            + [
                pl.BlockSpec((keys, HEAD), lambda g, _: (0, g // 2)),
                pl.BlockSpec((vt.shape[0], HEAD, QUARTER), lambda g, _: (0, g // 2, 0)),
            ]
            + [pl.BlockSpec((share, HEAD), lambda g, _: (0, g // 2))] * 2,
            out_specs=[pl.BlockSpec(half.shape, lambda g, _: (0, 0))] * 2,
            scratch_shapes=[
                pltpu.VMEM((width // HEAD, 8 * rows), F32),
                pltpu.VMEM((STEP_HEADS // 2, 16 * rows), F32),
            ],
        ),
        out_shape=[half, half],
        compiler_params=pltpu.CompilerParams(vmem_limit_bytes=MIDDLE),
        name="query_part",
    )(lengths, *pieces, k, vt, kq, vq)


def merge_kernel(count, roll, last, *refs):
    parts, outs = refs[:count], refs[count:]
    rows = parts[0].shape[0]
    heads = parts[0].shape[1] // HEAD - 1
    at = heads * HEAD
    lane = lax.broadcasted_iota(jnp.int32, (rows, LANES), 1)
    source = lax.broadcasted_iota(jnp.int32, (LANES, LANES), 0)
    columns = jnp.zeros((rows, LANES), F32)
    each = outs[0].shape[0]
    starts = [i * each % rows for i in range(len(outs))]
    block = rows // 4

    def turned(value, back):
        if not roll or back == 0:
            return value
        cut = rows - back * block
        return jnp.concatenate([value[cut:, :], value[:cut, :]], axis=0)

    logs = [part[:, at : at + LANES].astype(BF16) for part in parts]
    for h in range(heads):
        pick = ((source == h) | (source == heads + h) | (source == 2 * heads + h)).astype(F32)
        pick = pick.astype(BF16)
        log = [
            turned(jnp.dot(c, pick, preferred_element_type=F32), i) for i, c in enumerate(logs)
        ]
        top = functools.reduce(jnp.maximum, log)
        weights = [jnp.exp2(value - top) for value in log]
        total = functools.reduce(jnp.add, weights)
        merged = functools.reduce(
            jnp.add,
            [
                w * turned(part[:, h * HEAD : (h + 1) * HEAD].astype(F32), i)
                for i, (w, part) in enumerate(zip(weights, parts))
            ],
        )
        merged = merged / total
        for begin, out in zip(starts, outs):
            out[:, h * HEAD : (h + 1) * HEAD] = merged[begin : begin + each, :].astype(out.dtype)
        if not last:
            hi, mid, lo = split3(top + jnp.log(total) * math.log2(math.e))
            columns = jnp.where(lane == h, hi, columns)
            columns = jnp.where(lane == heads + h, mid, columns)
            columns = jnp.where(lane == 2 * heads + h, lo, columns)
    if not last:
        for begin, out in zip(starts, outs):
            out[:, at : at + LANES] = columns[begin : begin + each, :].astype(out.dtype)


def merge(parts, rows, types, roll=False, last=False, name="merge"):
    width = parts[0].shape[1] - (LANES if last else 0)
    whole = pl.BlockSpec(memory_space=pltpu.VMEM)
    return pl.pallas_call(
        functools.partial(merge_kernel, len(parts), roll, last),
        in_specs=[whole] * len(parts),
        out_specs=[whole] * len(types),
        out_shape=[jax.ShapeDtypeStruct((rows, width), t) for t in types],
        compiler_params=pltpu.CompilerParams(vmem_limit_bytes=16 << 20),
        name=name,
    )(*parts)


def project_kernel(*refs):
    pieces, w, outs, whole = refs[:8], refs[8], refs[9:13], refs[13]
    rows = pieces[0].shape[0]
    attn = jnp.concatenate([piece[...] for piece in pieces], axis=0)
    product = jnp.dot(attn, w[...], preferred_element_type=F32)
    block = rows // 4
    host, z, x, core = place()
    tensor = lax.axis_index("tensor")
    for i in range(8):
        home_core = (core + i // 4) & 1
        home_z = (z + 4 - i % 4) & 3
        for j in range(4):
            home_x = (x + 4 - j) & 3
            at = pl.multiple_of(((home_z * 4 + home_x) * 2 + home_core) * block, block)
            start = i * rows + j * block
            whole[pl.ds(at, block), :] = product[start : start + block, :]
    each = outs[0].shape[0]
    for ahead, out in enumerate(outs):
        at = pl.multiple_of(((tensor + ahead) & 3) * each, each)
        out[...] = whole[pl.ds(at, each), :]


def project(pieces, w):
    rows = 8 * pieces[0].shape[0]
    whole = pl.BlockSpec(memory_space=pltpu.VMEM)
    return pl.pallas_call(
        project_kernel,
        in_specs=[whole] * 9,
        out_specs=[whole] * 4,
        scratch_shapes=[pltpu.VMEM((rows, w.shape[1]), F32)],
        out_shape=[jax.ShapeDtypeStruct((rows // 4, w.shape[1]), F32)] * 4,
        compiler_params=pltpu.CompilerParams(vmem_limit_bytes=16 << 20),
        name="project",
    )(*pieces, w)


def host_at(z, x, core):
    return ((z % 4) * 4 + x % 4) * 2 + core


def moved(dz, dx, swap=0, cores=(0, 1)):
    return [
        (host_at(z, x, c), host_at(z + dz, x + dx, c ^ swap))
        for z in range(4)
        for x in range(4)
        for c in cores
    ]


def send(value, perm):
    return lax.ppermute(value, "hst", perm)


def after(value, *others):
    return lax.optimization_barrier((value, *others))[0]


def shards(cq, ck, cv, qq, qk, qv, w, lengths):
    host, z, x, core = place()
    by_x = {d: send(qq, moved(0, d)) for d in (1, 3, 2)}
    vt = turn(cv)
    keys_or_values = jnp.where(core == 0, ck, send(vt.reshape(ck.shape), [(0, 1)]))
    first_leg = {
        d: send(keys_or_values, [(0, host_at(d, 0, 0)), (1, host_at(0, d, 1))]) for d in (1, 3, 2)
    }
    row_q = jnp.concatenate([qq] + [after(by_x[d], keys_or_values) for d in (1, 2, 3)], axis=0)
    by_z = {d: send(row_q, moved(d, 0)) for d in (1, 3, 2)}
    tile1 = local_part(1, after(lengths, row_q, keys_or_values), cq, ck, vt)
    along = jnp.where(core == 0, z, x)
    line = keys_or_values
    for d in (1, 3, 2):
        line = jnp.where(along == d, after(first_leg[d], tile1[1]), line)
    second_leg = {
        d: send(
            line,
            [(host_at(i, 0, 0), host_at(i, d, 0)) for i in range(4)]
            + [(host_at(0, i, 1), host_at(d, i, 1)) for i in range(4)],
        )
        for d in (1, 3, 2)
    }
    by_z = [row_q] + [after(by_z[d], tile1[1]) for d in (1, 2, 3)]
    tile0 = local_part(0, after(lengths, line, *by_z), cq, ck, vt)
    pieces = by_z + [after(send(piece, moved(0, 0, 1)), tile0[1]) for piece in by_z]
    near, far = query_part(lengths, pieces, ck, vt, qk, qv)
    other = send(far, moved(0, 0, 1))
    across = jnp.where(core == 0, x, z)
    plane = line
    for d in (1, 3, 2):
        plane = jnp.where(across == d, after(second_leg[d], near), plane)
    swapped = send(plane, moved(0, 0, 1))
    dz = merge([near, other], near.shape[0] // 4, [F32, BF16, BF16, BF16], name="merge_core")
    from_z = [send(dz[d], moved(-d, 0)) for d in (1, 3, 2)]
    anchor_k = jnp.where(core == 0, plane, swapped)
    anchor_vt = jnp.where(core == 0, swapped, plane).reshape(vt.shape)
    out = anchor_part(1, 0, 2, after(lengths, dz[0]), cq, anchor_k, anchor_vt, *tile1, None)
    own_q, mine_q = merge(
        [dz[0], *(after(p, out) for p in from_z)], dz[0].shape[0], [F32, BF16], name="merge_z"
    )
    from_x = [send(mine_q, moved(0, d)) for d in (1, 2, 3)]
    out = anchor_part(1, 2, 2, after(lengths, mine_q), cq, anchor_k, anchor_vt, *tile1, out)
    (attn,) = merge(
        [own_q, *(after(p, out) for p in from_x)], own_q.shape[0], [BF16], True, True, "merge_x"
    )
    others = [send(attn, moved(d, 0)) for d in (1, 2, 3)]
    out = anchor_part(0, 0, 2, after(lengths, attn), cq, anchor_k, anchor_vt, *tile0, out)
    attn_z = [attn] + [after(p, out) for p in others]
    attn_all = attn_z + [send(piece, moved(0, 0, 1)) for piece in attn_z]
    sums = project(attn_all, w)
    swaps = [
        lax.ppermute(sums[d], "tensor", [(i, (i + d) % 4) for i in range(4)]) for d in (1, 2, 3)
    ]
    out = anchor_part(0, 2, 2, after(lengths, sums[0]), cq, anchor_k, anchor_vt, *tile0, out)
    query_out = (sums[0] + swaps[0] + swaps[1] + swaps[2]).astype(BF16)
    return out, query_out


def solution(mesh):
    in_specs = (
        P("hst", "tensor"),
        P("hst", "tensor"),
        P("hst", "tensor"),
        P("hst", "tensor"),
        P("hst", "tensor"),
        P("hst", "tensor"),
        P("tensor", "hst"),
        P(),
    )
    out_specs = (P("hst", "tensor"), P("tensor", "hst"))
    return jax.shard_map(shards, mesh=mesh, in_specs=in_specs, out_specs=out_specs, check_vma=False)
```

```python
import functools
import math

import jax
import jax.numpy as jnp
from jax import lax
from jax.experimental import pallas as pl
from jax.experimental.pallas import tpu as pltpu
from jax.sharding import PartitionSpec as P

HEAD = 128
SCALE = math.log2(math.e) / math.sqrt(HEAD)
MASKED = -1e30
SAFE = 2.0**100
TILE = 512
STEP_HEADS = 4
NT = (((1,), (1,)), ((), ()))
LANES = 128
F32 = jnp.float32
BF16 = jnp.bfloat16

QUARTER = 256
BIG = 60 << 20
MIDDLE = 32 << 20


def place():
    host = lax.axis_index("hst")
    return host, host >> 3, (host >> 1) & 3, host & 1


def scores(keys, queries):
    return lax.dot_general(keys, queries, NT, preferred_element_type=F32)


def weigh(s, shift):
    return jnp.exp2((s - shift) * SCALE)


def mix(values_t, probs):
    return jnp.dot(values_t, probs.astype(BF16), preferred_element_type=F32)


def exact_update(s, values_t, state):
    top, total, acc = state
    new_top = jnp.maximum(top, jnp.max(s, axis=0, keepdims=True))
    probs, old = weigh(s, new_top), weigh(top, new_top)
    return (
        new_top,
        total * old + jnp.sum(probs, axis=0, keepdims=True),
        acc * old + mix(values_t, probs),
    )


def fresh(rows):
    return (
        jnp.full((1, rows), MASKED, F32),
        jnp.zeros((1, rows), F32),
        jnp.zeros((HEAD, rows), F32),
    )


def below(limit, start, count):
    key = start + lax.broadcasted_iota(jnp.int32, (count, limit.shape[1]), 0)
    return key <= limit


def turn_kernel(v, out):
    for j in range(out.shape[0]):
        out[j] = v[j * QUARTER : (j + 1) * QUARTER, :].astype(F32).T.astype(BF16)


def turn(v):
    quarters = v.shape[0] // QUARTER
    whole = pl.BlockSpec(memory_space=pltpu.VMEM)
    return pl.pallas_call(
        turn_kernel,
        in_specs=[whole],
        out_specs=whole,
        out_shape=jax.ShapeDtypeStruct((quarters, v.shape[1], QUARTER), BF16),
        compiler_params=pltpu.CompilerParams(vmem_limit_bytes=16 << 20),
        name="turn",
    )(v)


def beside(vt, first, count):
    parts = [vt[j, :, :] for j in range(first, first + count)]
    return parts[0] if count == 1 else jnp.concatenate(parts, axis=1)


def local_kernel(tile, lengths, q, k, vt, acc, stats):
    keys = (tile + 1) * TILE
    half = QUARTER
    heads = q.shape[1] // HEAD
    own = lengths[place()[0]]
    row = tile * TILE + lax.broadcasted_iota(jnp.int32, (1, TILE), 1)
    limit = jnp.minimum(row, own - 1)
    wide = keys - half

    def score(h):
        query = q[:, h * HEAD : (h + 1) * HEAD]
        s = scores(k[0:wide, :], query)
        late = scores(k[wide:keys, :], query[half:, :])
        return s, late

    pending = score(0)
    for h in range(heads):
        s, late = pending
        if h + 1 < heads:
            pending = score(h + 1)
        shift = s[0:1, :]
        p = weigh(jnp.where(below(limit, 0, wide), s, MASKED), shift)
        p_late = weigh(
            jnp.where(below(limit[:, half:], wide, half), late, MASKED), shift[:, half:]
        )
        total = jnp.sum(p, axis=0, keepdims=True)
        total_late = jnp.sum(p_late, axis=0, keepdims=True)
        stats[0, h : h + 1, 0:half] = total[:, :half]
        stats[0, h : h + 1, half:] = total[:, half:] + total_late
        stats[0, STEP_HEADS + h : STEP_HEADS + h + 1, :] = shift
        o = mix(beside(vt, 0, wide // half), p)
        o_late = mix(vt[wide // half, :, :], p_late)
        acc[0, h, :, 0:half] = o[:, :half]
        acc[0, h, :, half:] = o[:, half:] + o_late

    @pl.when(jnp.logical_not(jnp.max(stats[0, 0:STEP_HEADS, :]) < SAFE))
    def _():
        for h in range(heads):
            query = q[:, h * HEAD : (h + 1) * HEAD]

            def chunk(j, state):
                at = pl.multiple_of(j * half, half)
                s = scores(k[pl.ds(at, half), :], query)
                s = jnp.where(below(limit, at, half), s, MASKED)
                return exact_update(s, vt[j], state)

            top, total, o = lax.fori_loop(0, keys // half, chunk, fresh(TILE))
            stats[0, h : h + 1, :] = total
            stats[0, STEP_HEADS + h : STEP_HEADS + h + 1, :] = top
            acc[0, h] = o


def local_part(tile, lengths, q, k, vt):
    keys = (tile + 1) * TILE
    heads = STEP_HEADS
    steps = q.shape[1] // (heads * HEAD)
    return pl.pallas_call(
        functools.partial(local_kernel, tile),
        grid_spec=pltpu.PrefetchScalarGridSpec(
            num_scalar_prefetch=1,
            grid=(steps,),
            in_specs=[
                pl.BlockSpec((TILE, heads * HEAD), lambda g, _: (tile, g)),
                pl.BlockSpec((keys, HEAD), lambda g, _: (0, g // 2)),
                pl.BlockSpec((keys // QUARTER, HEAD, QUARTER), lambda g, _: (0, g // 2, 0)),
            ],
            out_specs=[
                pl.BlockSpec((1, STEP_HEADS, HEAD, TILE), lambda g, _: (g, 0, 0, 0)),
                pl.BlockSpec((1, 2 * STEP_HEADS, TILE), lambda g, _: (g, 0, 0)),
            ],
        ),
        out_shape=[
            jax.ShapeDtypeStruct((steps, STEP_HEADS, HEAD, TILE), F32),
            jax.ShapeDtypeStruct((steps, 2 * STEP_HEADS, TILE), F32),
        ],
        compiler_params=pltpu.CompilerParams(vmem_limit_bytes=BIG),
        name=f"local_{tile}",
    )(lengths, q, k, vt)


def anchor_kernel(lengths, q, k, vt, acc, stats, *rest):
    out, totals = rest[-2:]
    n = jnp.where(place()[0] > 0, lengths[0], 0)
    quarters = (n + QUARTER - 1) // QUARTER
    limit = jnp.full((1, TILE), n - 1, jnp.int32)

    def finish(h, o, total):
        out[:, h * HEAD : (h + 1) * HEAD] = (o * (1.0 / total)).T.astype(BF16)

    def query(h):
        return q[:, h * HEAD : (h + 1) * HEAD]

    @pl.when(quarters == 0)
    def _():
        totals[...] = stats[0, 0:STEP_HEADS, :]
        for h in range(STEP_HEADS):
            finish(h, acc[0, h], stats[0, h : h + 1, :])

    def run(count):
        near = (count - 1) * QUARTER

        def score(h):
            late = scores(k[near : near + QUARTER, :], query(h))
            return late if near == 0 else (scores(k[0:near, :], query(h)), late)

        pending = score(0)
        for h in range(STEP_HEADS):
            s = pending
            if h + 1 < STEP_HEADS:
                pending = score(h + 1)
            shift = stats[0, STEP_HEADS + h : STEP_HEADS + h + 1, :]
            late = s if near == 0 else s[1]
            p = weigh(jnp.where(below(limit, near, QUARTER), late, MASKED), shift)
            total = stats[0, h : h + 1, :] + jnp.sum(p, axis=0, keepdims=True)
            p = p.astype(BF16)
            if near:
                p_near = weigh(s[0], shift)
                total = total + jnp.sum(p_near, axis=0, keepdims=True)
                p = jnp.concatenate([p_near.astype(BF16), p], axis=0)
            totals[h : h + 1, :] = total
            finish(h, acc[0, h] + mix(beside(vt, 0, count), p), total)

    for count in range(1, vt.shape[0] + 1):
        pl.when(quarters == count)(functools.partial(run, count))

    @pl.when(jnp.logical_not(jnp.max(totals[...]) < SAFE))
    def _():
        for h in range(STEP_HEADS):

            def chunk(j, state):
                at = pl.multiple_of(j * QUARTER, QUARTER)
                s = scores(k[pl.ds(at, QUARTER), :], query(h))
                s = jnp.where(below(limit, at, QUARTER), s, MASKED)
                return exact_update(s, vt[j], state)

            begin = (
                stats[0, STEP_HEADS + h : STEP_HEADS + h + 1, :],
                stats[0, h : h + 1, :],
                acc[0, h],
            )
            top, total, o = lax.fori_loop(0, quarters, chunk, begin)
            finish(h, o, total)


def anchor_part(tile, first, steps, lengths, q, k, vt, acc, stats, out):
    wide = STEP_HEADS * HEAD
    in_specs = [
        pl.BlockSpec((TILE, wide), lambda s, _: (tile, first + s)),
        pl.BlockSpec((k.shape[0], HEAD), lambda s, _: (0, (first + s) // 2)),
        pl.BlockSpec((vt.shape[0], HEAD, QUARTER), lambda s, _: (0, (first + s) // 2, 0)),
        pl.BlockSpec((1, STEP_HEADS, HEAD, TILE), lambda s, _: (first + s, 0, 0, 0)),
        pl.BlockSpec((1, 2 * STEP_HEADS, TILE), lambda s, _: (first + s, 0, 0)),
    ]
    args = [lengths, q, k, vt, acc, stats]
    aliases = {}
    if out is not None:
        in_specs.append(pl.BlockSpec(memory_space=pl.ANY))
        aliases = {len(args): 0}
        args.append(out)
    return pl.pallas_call(
        anchor_kernel,
        grid_spec=pltpu.PrefetchScalarGridSpec(
            num_scalar_prefetch=1,
            grid=(steps,),
            in_specs=in_specs,
            out_specs=pl.BlockSpec((TILE, wide), lambda s, _: (tile, first + s)),
            scratch_shapes=[pltpu.VMEM((STEP_HEADS, TILE), F32)],
        ),
        out_shape=jax.ShapeDtypeStruct(q.shape, BF16),
        input_output_aliases=aliases,
        compiler_params=pltpu.CompilerParams(vmem_limit_bytes=BIG),
        name=f"anchor_{tile}_{first}",
    )(*args)


def split3(value):
    hi = value.astype(BF16).astype(F32)
    mid = (value - hi).astype(BF16).astype(F32)
    return hi, mid, value - hi - mid


def query_kernel(lengths, *refs):
    pieces, (k, vt, kq, vq, near, far, lse, totals) = refs[:-8], refs[-8:]
    step = pl.program_id(0)
    rows = len(pieces) * pieces[0].shape[0]
    half = rows // 2
    wide = 2 * rows
    keys = k.shape[0]
    share = kq.shape[0]
    host, z, x, core = place()
    lane = lax.broadcasted_iota(jnp.int32, (1, wide), 1)
    home_x = (x + 4 - ((lane >> 3) & 3)) & 3
    home_z = z ^ ((lane >> 5) & 3)
    home_core = (core + ((lane >> 7) & 1)) & 1
    row = ((home_z * 4 + home_x) * 2 + home_core) * share + (lane & 7)
    limit = jnp.full((1, wide), lengths[host] - 1, jnp.int32)
    late_limit = jnp.minimum(row - host * share, share - 1)
    query_keys = jnp.concatenate(
        [kq[...].astype(F32), jnp.zeros((16 - share, HEAD), F32)], axis=0
    ).astype(BF16)
    query_values = jnp.concatenate(
        [vq[...].astype(F32), jnp.zeros((LANES - share, HEAD), F32)], axis=0
    ).T[:, 0:16].astype(BF16)

    def pair(a):
        parts = [piece[:, h * HEAD : (h + 1) * HEAD] for h in (2 * a, 2 * a + 1) for piece in pieces]
        return jnp.concatenate(parts, axis=0)

    def late_score(query):
        return jnp.where(below(late_limit, 0, 16), scores(query_keys, query), MASKED)

    def score(a):
        query = pair(a)
        return scores(k[...], query), late_score(query)

    def finish(a, o, total, top):
        totals[a : a + 1, :] = total
        o = o * (1.0 / total)
        log_total = top * SCALE + jnp.log(total) * math.log2(math.e)
        for b in range(2):
            h = step * STEP_HEADS + 2 * a + b
            lse[pl.ds(h, 1), :] = log_total[:, b * rows : (b + 1) * rows]
            at = pl.multiple_of(h * HEAD, HEAD)
            o_rows = o[:, b * rows : (b + 1) * rows].T
            near[:, pl.ds(at, HEAD)] = o_rows[:half, :]
            far[:, pl.ds(at, HEAD)] = o_rows[half:, :]

    values = beside(vt, 0, keys // QUARTER)
    pending = score(0)
    for a in range(STEP_HEADS // 2):
        s, late = pending
        if a + 1 < STEP_HEADS // 2:
            pending = score(a + 1)
        shift = s[0:1, :]
        p = weigh(jnp.where(below(limit, 0, keys), s, MASKED), shift)
        p_late = weigh(late, shift)
        total = jnp.sum(p, axis=0, keepdims=True) + jnp.sum(p_late, axis=0, keepdims=True)
        finish(a, mix(values, p) + mix(query_values, p_late), total, shift)

    @pl.when(jnp.logical_not(jnp.max(totals[...]) < SAFE))
    def _():
        for a in range(STEP_HEADS // 2):
            query = pair(a)

            def chunk(j, state):
                at = pl.multiple_of(j * QUARTER, QUARTER)
                s = scores(k[pl.ds(at, QUARTER), :], query)
                s = jnp.where(below(limit, at, QUARTER), s, MASKED)
                return exact_update(s, vt[j], state)

            state = lax.fori_loop(0, keys // QUARTER, chunk, fresh(wide))
            top, total, o = exact_update(late_score(query), query_values, state)
            finish(a, o, total, top)

    @pl.when(step == pl.num_programs(0) - 1)
    def _():
        count = lse.shape[0]
        parts = split3(lse[...])
        columns = jnp.concatenate(
            [*parts, jnp.zeros((LANES - 3 * count, rows), F32)], axis=0
        ).T
        at = count * HEAD
        near[:, at : at + LANES] = columns[:half, :]
        far[:, at : at + LANES] = columns[half:, :]


def query_part(lengths, pieces, k, vt, kq, vq):
    each, width = pieces[0].shape
    rows = each * len(pieces)
    keys = k.shape[0]
    share = kq.shape[0]
    half = jax.ShapeDtypeStruct((rows // 2, width + LANES), F32)
    return pl.pallas_call(
        query_kernel,
        grid_spec=pltpu.PrefetchScalarGridSpec(
            num_scalar_prefetch=1,
            grid=(width // (STEP_HEADS * HEAD),),
            in_specs=[pl.BlockSpec((each, STEP_HEADS * HEAD), lambda g, _: (0, g))] * len(pieces)
            + [
                pl.BlockSpec((keys, HEAD), lambda g, _: (0, g // 2)),
                pl.BlockSpec((vt.shape[0], HEAD, QUARTER), lambda g, _: (0, g // 2, 0)),
            ]
            + [pl.BlockSpec((share, HEAD), lambda g, _: (0, g // 2))] * 2,
            out_specs=[pl.BlockSpec(half.shape, lambda g, _: (0, 0))] * 2,
            scratch_shapes=[
                pltpu.VMEM((width // HEAD, rows), F32),
                pltpu.VMEM((STEP_HEADS // 2, 2 * rows), F32),
            ],
        ),
        out_shape=[half, half],
        compiler_params=pltpu.CompilerParams(vmem_limit_bytes=MIDDLE),
        name="query_part",
    )(lengths, *pieces, k, vt, kq, vq)


def merge_kernel(count, roll, last, *refs):
    parts, outs = refs[:count], refs[count:]
    rows = parts[0].shape[0]
    heads = parts[0].shape[1] // HEAD - 1
    at = heads * HEAD
    lane = lax.broadcasted_iota(jnp.int32, (rows, LANES), 1)
    source = lax.broadcasted_iota(jnp.int32, (LANES, LANES), 0)
    columns = jnp.zeros((rows, LANES), F32)
    each = outs[0].shape[0]
    starts = [i * each % rows for i in range(len(outs))]
    block = rows // 4

    def turned(value, back):
        if not roll or back == 0:
            return value
        cut = rows - back * block
        return jnp.concatenate([value[cut:, :], value[:cut, :]], axis=0)

    logs = [part[:, at : at + LANES].astype(BF16) for part in parts]
    for h in range(heads):
        pick = ((source == h) | (source == heads + h) | (source == 2 * heads + h)).astype(F32)
        pick = pick.astype(BF16)
        log = [
            turned(jnp.dot(c, pick, preferred_element_type=F32), i) for i, c in enumerate(logs)
        ]
        top = functools.reduce(jnp.maximum, log)
        weights = [jnp.exp2(value - top) for value in log]
        total = functools.reduce(jnp.add, weights)
        merged = functools.reduce(
            jnp.add,
            [
                w * turned(part[:, h * HEAD : (h + 1) * HEAD].astype(F32), i)
                for i, (w, part) in enumerate(zip(weights, parts))
            ],
        )
        merged = merged / total
        for begin, out in zip(starts, outs):
            out[:, h * HEAD : (h + 1) * HEAD] = merged[begin : begin + each, :].astype(out.dtype)
        if not last:
            hi, mid, lo = split3(top + jnp.log(total) * math.log2(math.e))
            columns = jnp.where(lane == h, hi, columns)
            columns = jnp.where(lane == heads + h, mid, columns)
            columns = jnp.where(lane == 2 * heads + h, lo, columns)
    if not last:
        for begin, out in zip(starts, outs):
            out[:, at : at + LANES] = columns[begin : begin + each, :].astype(out.dtype)


def merge(parts, rows, types, roll=False, last=False, name="merge"):
    width = parts[0].shape[1] - (LANES if last else 0)
    whole = pl.BlockSpec(memory_space=pltpu.VMEM)
    return pl.pallas_call(
        functools.partial(merge_kernel, len(parts), roll, last),
        in_specs=[whole] * len(parts),
        out_specs=[whole] * len(types),
        out_shape=[jax.ShapeDtypeStruct((rows, width), t) for t in types],
        compiler_params=pltpu.CompilerParams(vmem_limit_bytes=16 << 20),
        name=name,
    )(*parts)


def project_kernel(*refs):
    pieces, w, outs, whole = refs[:8], refs[8], refs[9:13], refs[13]
    rows = pieces[0].shape[0]
    attn = jnp.concatenate([piece[...] for piece in pieces], axis=0)
    product = jnp.dot(attn, w[...], preferred_element_type=F32)
    block = rows // 4
    host, z, x, core = place()
    tensor = lax.axis_index("tensor")
    for i in range(8):
        home_core = (core + i // 4) & 1
        home_z = z ^ (i % 4)
        for j in range(4):
            home_x = (x + 4 - j) & 3
            at = pl.multiple_of(((home_z * 4 + home_x) * 2 + home_core) * block, block)
            start = i * rows + j * block
            whole[pl.ds(at, block), :] = product[start : start + block, :]
    each = outs[0].shape[0]
    for ahead, out in enumerate(outs):
        at = pl.multiple_of(((tensor + ahead) & 3) * each, each)
        out[...] = whole[pl.ds(at, each), :]


def project(pieces, w):
    rows = 8 * pieces[0].shape[0]
    whole = pl.BlockSpec(memory_space=pltpu.VMEM)
    return pl.pallas_call(
        project_kernel,
        in_specs=[whole] * 9,
        out_specs=[whole] * 4,
        scratch_shapes=[pltpu.VMEM((rows, w.shape[1]), F32)],
        out_shape=[jax.ShapeDtypeStruct((rows // 4, w.shape[1]), F32)] * 4,
        compiler_params=pltpu.CompilerParams(vmem_limit_bytes=16 << 20),
        name="project",
    )(*pieces, w)


def host_at(z, x, core):
    return ((z % 4) * 4 + x % 4) * 2 + core


def moved(dz, dx, swap=0, cores=(0, 1)):
    return [
        (host_at(z, x, c), host_at(z + dz, x + dx, c ^ swap))
        for z in range(4)
        for x in range(4)
        for c in cores
    ]


def crossed(dz):
    return [
        (host_at(z, x, c), host_at(z ^ dz, x, c))
        for z in range(4)
        for x in range(4)
        for c in (0, 1)
    ]


def spread(steps):
    first = [(host_at(i, a, 0), host_at(i, b, 0)) for i in range(4) for a, b in steps]
    return first + [(host_at(a, i, 1), host_at(b, i, 1)) for i in range(4) for a, b in steps]


def send(value, perm):
    return lax.ppermute(value, "hst", perm)


def after(value, *others):
    return lax.optimization_barrier((value, *others))[0]


def shards(cq, ck, cv, qq, qk, qv, w, lengths):
    host, z, x, core = place()
    by_x = {d: send(qq, moved(0, d)) for d in (1, 3, 2)}
    vt = turn(cv)
    keys_or_values = jnp.where(core == 0, ck, send(vt.reshape(ck.shape), [(0, 1)]))
    row_q = jnp.concatenate([qq] + [after(by_x[d], vt) for d in (1, 2, 3)], axis=0)
    next_q = send(row_q, crossed(1))
    keys_or_values = after(keys_or_values, row_q)
    first_leg = {
        d: send(keys_or_values, [(0, host_at(d, 0, 0)), (1, host_at(0, d, 1))]) for d in (1, 3, 2)
    }
    tile1 = local_part(1, after(lengths, row_q, keys_or_values), cq, ck, vt)
    pair_q = jnp.concatenate([row_q, after(next_q, tile1[1])], axis=0)
    other_q = send(pair_q, crossed(2))
    along = jnp.where(core == 0, z, x)
    line = keys_or_values
    for d in (1, 3, 2):
        line = jnp.where(along == d, after(first_leg[d], tile1[1]), line)
    across = jnp.where(core == 0, x, z)
    third = send(line, spread([(0, 1)]))
    tile0 = local_part(0, after(lengths, line, pair_q), cq, ck, vt)
    far_q = send(pair_q, moved(0, 0, 1))
    other_q = after(other_q, tile0[1])
    pieces = [pair_q, other_q, after(far_q, tile0[1]), send(other_q, moved(0, 0, 1))]
    line = jnp.where(across == 1, after(third, tile0[1]), line)
    fourth = send(line, spread([(0, 3), (1, 2)]))
    near, far = query_part(after(lengths, line), pieces, ck, vt, qk, qv)
    other = send(far, moved(0, 0, 1))
    plane = jnp.where(across >= 2, after(fourth, near), line)
    swapped = send(plane, moved(0, 0, 1))
    dz = merge([near, other], near.shape[0] // 4, [F32, BF16, BF16, BF16], name="merge_core")
    from_z = [send(dz[d], crossed(d)) for d in (1, 3, 2)]
    anchor_k = jnp.where(core == 0, plane, swapped)
    anchor_vt = jnp.where(core == 0, swapped, plane).reshape(vt.shape)
    out = anchor_part(1, 0, 2, after(lengths, dz[0]), cq, anchor_k, anchor_vt, *tile1, None)
    own_q, mine_q = merge(
        [dz[0], *(after(p, out) for p in from_z)], dz[0].shape[0], [F32, BF16], name="merge_z"
    )
    from_x = [send(mine_q, moved(0, d)) for d in (1, 2, 3)]
    out = anchor_part(1, 2, 2, after(lengths, mine_q), cq, anchor_k, anchor_vt, *tile1, out)
    (attn,) = merge(
        [own_q, *(after(p, out) for p in from_x)], own_q.shape[0], [BF16], True, True, "merge_x"
    )
    others = [send(attn, crossed(d)) for d in (1, 2, 3)]
    out = anchor_part(0, 0, 2, after(lengths, attn), cq, anchor_k, anchor_vt, *tile0, out)
    attn_z = [attn] + [after(p, out) for p in others]
    attn_all = attn_z + [send(piece, moved(0, 0, 1)) for piece in attn_z]
    sums = project(attn_all, w)
    swaps = [
        lax.ppermute(sums[d], "tensor", [(i, (i + d) % 4) for i in range(4)]) for d in (1, 2, 3)
    ]
    out = anchor_part(0, 2, 2, after(lengths, sums[0]), cq, anchor_k, anchor_vt, *tile0, out)
    query_out = (sums[0] + swaps[0] + swaps[1] + swaps[2]).astype(BF16)
    return out, query_out


def solution(mesh):
    in_specs = (
        P("hst", "tensor"),
        P("hst", "tensor"),
        P("hst", "tensor"),
        P("hst", "tensor"),
        P("hst", "tensor"),
        P("hst", "tensor"),
        P("tensor", "hst"),
        P(),
    )
    out_specs = (P("hst", "tensor"), P("tensor", "hst"))
    return jax.shard_map(shards, mesh=mesh, in_specs=in_specs, out_specs=out_specs, check_vma=False)
```

```python
import functools
import math

import jax
import jax.numpy as jnp
from jax import lax
from jax.experimental import pallas as pl
from jax.experimental.pallas import tpu as pltpu
from jax.sharding import PartitionSpec as P

HEAD = 128
SCALE = math.log2(math.e) / math.sqrt(HEAD)
MASKED = -1e30
SAFE = 2.0**100
TILE = 512
STEP_HEADS = 4
NT = (((1,), (1,)), ((), ()))
LANES = 128
F32 = jnp.float32
BF16 = jnp.bfloat16

QUARTER = 256
BIG = 60 << 20
MIDDLE = 32 << 20


def place():
    host = lax.axis_index("hst")
    return host, host >> 3, (host >> 1) & 3, host & 1


def scores(keys, queries):
    return lax.dot_general(keys, queries, NT, preferred_element_type=F32)


def weigh(s, shift):
    return jnp.exp2((s - shift) * SCALE)


def mix(values_t, probs):
    return jnp.dot(values_t, probs.astype(BF16), preferred_element_type=F32)


def exact_update(s, values_t, state):
    top, total, acc = state
    new_top = jnp.maximum(top, jnp.max(s, axis=0, keepdims=True))
    probs, old = weigh(s, new_top), weigh(top, new_top)
    return (
        new_top,
        total * old + jnp.sum(probs, axis=0, keepdims=True),
        acc * old + mix(values_t, probs),
    )


def fresh(rows):
    return (
        jnp.full((1, rows), MASKED, F32),
        jnp.zeros((1, rows), F32),
        jnp.zeros((HEAD, rows), F32),
    )


def below(limit, start, count):
    key = start + lax.broadcasted_iota(jnp.int32, (count, limit.shape[1]), 0)
    return key <= limit


def turn_kernel(v, out):
    for j in range(out.shape[0]):
        out[j] = v[j * QUARTER : (j + 1) * QUARTER, :].astype(F32).T.astype(BF16)


def turn(v):
    quarters = v.shape[0] // QUARTER
    whole = pl.BlockSpec(memory_space=pltpu.VMEM)
    return pl.pallas_call(
        turn_kernel,
        in_specs=[whole],
        out_specs=whole,
        out_shape=jax.ShapeDtypeStruct((quarters, v.shape[1], QUARTER), BF16),
        compiler_params=pltpu.CompilerParams(vmem_limit_bytes=16 << 20),
        name="turn",
    )(v)


def beside(vt, first, count):
    parts = [vt[j, :, :] for j in range(first, first + count)]
    return parts[0] if count == 1 else jnp.concatenate(parts, axis=1)


def local_kernel(tile, lengths, q, k, vt, acc, stats):
    keys = (tile + 1) * TILE
    half = QUARTER
    heads = q.shape[1] // HEAD
    own = lengths[place()[0]]
    row = tile * TILE + lax.broadcasted_iota(jnp.int32, (1, TILE), 1)
    limit = jnp.minimum(row, own - 1)
    wide = keys - half

    def score(h):
        query = q[:, h * HEAD : (h + 1) * HEAD]
        s = scores(k[0:wide, :], query)
        late = scores(k[wide:keys, :], query[half:, :])
        return s, late

    pending = score(0)
    for h in range(heads):
        s, late = pending
        if h + 1 < heads:
            pending = score(h + 1)
        shift = s[0:1, :]
        p = weigh(jnp.where(below(limit, 0, wide), s, MASKED), shift)
        p_late = weigh(
            jnp.where(below(limit[:, half:], wide, half), late, MASKED), shift[:, half:]
        )
        total = jnp.sum(p, axis=0, keepdims=True)
        total_late = jnp.sum(p_late, axis=0, keepdims=True)
        stats[0, h : h + 1, 0:half] = total[:, :half]
        stats[0, h : h + 1, half:] = total[:, half:] + total_late
        stats[0, STEP_HEADS + h : STEP_HEADS + h + 1, :] = shift
        o = mix(beside(vt, 0, wide // half), p)
        o_late = mix(vt[wide // half, :, :], p_late)
        acc[0, h, :, 0:half] = o[:, :half]
        acc[0, h, :, half:] = o[:, half:] + o_late

    @pl.when(jnp.logical_not(jnp.max(stats[0, 0:STEP_HEADS, :]) < SAFE))
    def _():
        for h in range(heads):
            query = q[:, h * HEAD : (h + 1) * HEAD]

            def chunk(j, state):
                at = pl.multiple_of(j * half, half)
                s = scores(k[pl.ds(at, half), :], query)
                s = jnp.where(below(limit, at, half), s, MASKED)
                return exact_update(s, vt[j], state)

            top, total, o = lax.fori_loop(0, keys // half, chunk, fresh(TILE))
            stats[0, h : h + 1, :] = total
            stats[0, STEP_HEADS + h : STEP_HEADS + h + 1, :] = top
            acc[0, h] = o


def local_part(tile, lengths, q, k, vt):
    keys = (tile + 1) * TILE
    heads = STEP_HEADS
    steps = q.shape[1] // (heads * HEAD)
    return pl.pallas_call(
        functools.partial(local_kernel, tile),
        grid_spec=pltpu.PrefetchScalarGridSpec(
            num_scalar_prefetch=1,
            grid=(steps,),
            in_specs=[
                pl.BlockSpec((TILE, heads * HEAD), lambda g, _: (tile, g)),
                pl.BlockSpec((keys, HEAD), lambda g, _: (0, g // 2)),
                pl.BlockSpec((keys // QUARTER, HEAD, QUARTER), lambda g, _: (0, g // 2, 0)),
            ],
            out_specs=[
                pl.BlockSpec((1, STEP_HEADS, HEAD, TILE), lambda g, _: (g, 0, 0, 0)),
                pl.BlockSpec((1, 2 * STEP_HEADS, TILE), lambda g, _: (g, 0, 0)),
            ],
        ),
        out_shape=[
            jax.ShapeDtypeStruct((steps, STEP_HEADS, HEAD, TILE), F32),
            jax.ShapeDtypeStruct((steps, 2 * STEP_HEADS, TILE), F32),
        ],
        compiler_params=pltpu.CompilerParams(vmem_limit_bytes=BIG),
        cost_estimate=pl.CostEstimate(flops=(tile + 1) * 4_000_000_000, bytes_accessed=8 << 20, transcendentals=0),
        name=f"local_{tile}",
    )(lengths, q, k, vt)


def anchor_kernel(lengths, q, k, vt, acc, stats, *rest):
    out, totals = rest[-2:]
    n = jnp.where(place()[0] > 0, lengths[0], 0)
    quarters = (n + QUARTER - 1) // QUARTER
    limit = jnp.full((1, TILE), n - 1, jnp.int32)

    def finish(h, o, total):
        out[:, h * HEAD : (h + 1) * HEAD] = (o * (1.0 / total)).T.astype(BF16)

    def query(h):
        return q[:, h * HEAD : (h + 1) * HEAD]

    @pl.when(quarters == 0)
    def _():
        totals[...] = stats[0, 0:STEP_HEADS, :]
        for h in range(STEP_HEADS):
            finish(h, acc[0, h], stats[0, h : h + 1, :])

    def run(count):
        near = (count - 1) * QUARTER

        def score(h):
            late = scores(k[near : near + QUARTER, :], query(h))
            return late if near == 0 else (scores(k[0:near, :], query(h)), late)

        pending = score(0)
        for h in range(STEP_HEADS):
            s = pending
            if h + 1 < STEP_HEADS:
                pending = score(h + 1)
            shift = stats[0, STEP_HEADS + h : STEP_HEADS + h + 1, :]
            late = s if near == 0 else s[1]
            p = weigh(jnp.where(below(limit, near, QUARTER), late, MASKED), shift)
            total = stats[0, h : h + 1, :] + jnp.sum(p, axis=0, keepdims=True)
            p = p.astype(BF16)
            if near:
                p_near = weigh(s[0], shift)
                total = total + jnp.sum(p_near, axis=0, keepdims=True)
                p = jnp.concatenate([p_near.astype(BF16), p], axis=0)
            totals[h : h + 1, :] = total
            finish(h, acc[0, h] + mix(beside(vt, 0, count), p), total)

    for count in range(1, vt.shape[0] + 1):
        pl.when(quarters == count)(functools.partial(run, count))

    @pl.when(jnp.logical_not(jnp.max(totals[...]) < SAFE))
    def _():
        for h in range(STEP_HEADS):

            def chunk(j, state):
                at = pl.multiple_of(j * QUARTER, QUARTER)
                s = scores(k[pl.ds(at, QUARTER), :], query(h))
                s = jnp.where(below(limit, at, QUARTER), s, MASKED)
                return exact_update(s, vt[j], state)

            begin = (
                stats[0, STEP_HEADS + h : STEP_HEADS + h + 1, :],
                stats[0, h : h + 1, :],
                acc[0, h],
            )
            top, total, o = lax.fori_loop(0, quarters, chunk, begin)
            finish(h, o, total)


def anchor_part(tile, first, steps, lengths, q, k, vt, acc, stats, out):
    wide = STEP_HEADS * HEAD
    in_specs = [
        pl.BlockSpec((TILE, wide), lambda s, _: (tile, first + s)),
        pl.BlockSpec((k.shape[0], HEAD), lambda s, _: (0, (first + s) // 2)),
        pl.BlockSpec((vt.shape[0], HEAD, QUARTER), lambda s, _: (0, (first + s) // 2, 0)),
        pl.BlockSpec((1, STEP_HEADS, HEAD, TILE), lambda s, _: (first + s, 0, 0, 0)),
        pl.BlockSpec((1, 2 * STEP_HEADS, TILE), lambda s, _: (first + s, 0, 0)),
    ]
    args = [lengths, q, k, vt, acc, stats]
    aliases = {}
    if out is not None:
        in_specs.append(pl.BlockSpec(memory_space=pl.ANY))
        aliases = {len(args): 0}
        args.append(out)
    return pl.pallas_call(
        anchor_kernel,
        grid_spec=pltpu.PrefetchScalarGridSpec(
            num_scalar_prefetch=1,
            grid=(steps,),
            in_specs=in_specs,
            out_specs=pl.BlockSpec((TILE, wide), lambda s, _: (tile, first + s)),
            scratch_shapes=[pltpu.VMEM((STEP_HEADS, TILE), F32)],
        ),
        out_shape=jax.ShapeDtypeStruct(q.shape, BF16),
        input_output_aliases=aliases,
        compiler_params=pltpu.CompilerParams(vmem_limit_bytes=BIG),
        cost_estimate=pl.CostEstimate(flops=4_000_000_000, bytes_accessed=8 << 20, transcendentals=0),
        name=f"anchor_{tile}_{first}",
    )(*args)


def split3(value):
    hi = value.astype(BF16).astype(F32)
    mid = (value - hi).astype(BF16).astype(F32)
    return hi, mid, value - hi - mid


def query_kernel(lengths, *refs):
    pieces, (k, vt, kq, vq, near, far, lse, totals) = refs[:-8], refs[-8:]
    step = pl.program_id(0)
    rows = len(pieces) * pieces[0].shape[0]
    half = rows // 2
    wide = 2 * rows
    keys = k.shape[0]
    share = kq.shape[0]
    host, z, x, core = place()
    lane = lax.broadcasted_iota(jnp.int32, (1, wide), 1)
    home_x = (x + 4 - ((lane >> 3) & 3)) & 3
    home_z = z ^ ((lane >> 5) & 3)
    home_core = (core + ((lane >> 7) & 1)) & 1
    row = ((home_z * 4 + home_x) * 2 + home_core) * share + (lane & 7)
    limit = jnp.full((1, wide), lengths[host] - 1, jnp.int32)
    late_limit = jnp.minimum(row - host * share, share - 1)
    query_keys = jnp.concatenate(
        [kq[...].astype(F32), jnp.zeros((16 - share, HEAD), F32)], axis=0
    ).astype(BF16)
    query_values = jnp.concatenate(
        [vq[...].astype(F32), jnp.zeros((LANES - share, HEAD), F32)], axis=0
    ).T[:, 0:16].astype(BF16)

    def pair(a):
        parts = [piece[:, h * HEAD : (h + 1) * HEAD] for h in (2 * a, 2 * a + 1) for piece in pieces]
        return jnp.concatenate(parts, axis=0)

    def late_score(query):
        return jnp.where(below(late_limit, 0, 16), scores(query_keys, query), MASKED)

    def score(a):
        query = pair(a)
        return scores(k[...], query), late_score(query)

    def finish(a, o, total, top):
        totals[a : a + 1, :] = total
        o = o * (1.0 / total)
        log_total = top * SCALE + jnp.log(total) * math.log2(math.e)
        for b in range(2):
            h = step * STEP_HEADS + 2 * a + b
            lse[pl.ds(h, 1), :] = log_total[:, b * rows : (b + 1) * rows]
            at = pl.multiple_of(h * HEAD, HEAD)
            o_rows = o[:, b * rows : (b + 1) * rows].T
            near[:, pl.ds(at, HEAD)] = o_rows[:half, :]
            far[:, pl.ds(at, HEAD)] = o_rows[half:, :]

    values = beside(vt, 0, keys // QUARTER)
    pending = score(0)
    for a in range(STEP_HEADS // 2):
        s, late = pending
        if a + 1 < STEP_HEADS // 2:
            pending = score(a + 1)
        shift = s[0:1, :]
        p = weigh(jnp.where(below(limit, 0, keys), s, MASKED), shift)
        p_late = weigh(late, shift)
        total = jnp.sum(p, axis=0, keepdims=True) + jnp.sum(p_late, axis=0, keepdims=True)
        finish(a, mix(values, p) + mix(query_values, p_late), total, shift)

    @pl.when(jnp.logical_not(jnp.max(totals[...]) < SAFE))
    def _():
        for a in range(STEP_HEADS // 2):
            query = pair(a)

            def chunk(j, state):
                at = pl.multiple_of(j * QUARTER, QUARTER)
                s = scores(k[pl.ds(at, QUARTER), :], query)
                s = jnp.where(below(limit, at, QUARTER), s, MASKED)
                return exact_update(s, vt[j], state)

            state = lax.fori_loop(0, keys // QUARTER, chunk, fresh(wide))
            top, total, o = exact_update(late_score(query), query_values, state)
            finish(a, o, total, top)

    @pl.when(step == pl.num_programs(0) - 1)
    def _():
        count = lse.shape[0]
        parts = split3(lse[...])
        columns = jnp.concatenate(
            [*parts, jnp.zeros((LANES - 3 * count, rows), F32)], axis=0
        ).T
        at = count * HEAD
        near[:, at : at + LANES] = columns[:half, :]
        far[:, at : at + LANES] = columns[half:, :]


def query_part(lengths, pieces, k, vt, kq, vq):
    each, width = pieces[0].shape
    rows = each * len(pieces)
    keys = k.shape[0]
    share = kq.shape[0]
    half = jax.ShapeDtypeStruct((rows // 2, width + LANES), F32)
    return pl.pallas_call(
        query_kernel,
        grid_spec=pltpu.PrefetchScalarGridSpec(
            num_scalar_prefetch=1,
            grid=(width // (STEP_HEADS * HEAD),),
            in_specs=[pl.BlockSpec((each, STEP_HEADS * HEAD), lambda g, _: (0, g))] * len(pieces)
            + [
                pl.BlockSpec((keys, HEAD), lambda g, _: (0, g // 2)),
                pl.BlockSpec((vt.shape[0], HEAD, QUARTER), lambda g, _: (0, g // 2, 0)),
            ]
            + [pl.BlockSpec((share, HEAD), lambda g, _: (0, g // 2))] * 2,
            out_specs=[pl.BlockSpec(half.shape, lambda g, _: (0, 0))] * 2,
            scratch_shapes=[
                pltpu.VMEM((width // HEAD, rows), F32),
                pltpu.VMEM((STEP_HEADS // 2, 2 * rows), F32),
            ],
        ),
        out_shape=[half, half],
        compiler_params=pltpu.CompilerParams(vmem_limit_bytes=MIDDLE),
        cost_estimate=pl.CostEstimate(flops=5_000_000_000, bytes_accessed=4 << 20, transcendentals=0),
        name="query_part",
    )(lengths, *pieces, k, vt, kq, vq)


def merge_kernel(count, roll, last, *refs):
    parts, outs = refs[:count], refs[count:]
    rows = parts[0].shape[0]
    heads = parts[0].shape[1] // HEAD - 1
    at = heads * HEAD
    lane = lax.broadcasted_iota(jnp.int32, (rows, LANES), 1)
    source = lax.broadcasted_iota(jnp.int32, (LANES, LANES), 0)
    columns = jnp.zeros((rows, LANES), F32)
    each = outs[0].shape[0]
    starts = [i * each % rows for i in range(len(outs))]
    block = rows // 4

    def turned(value, back):
        if not roll or back == 0:
            return value
        cut = rows - back * block
        return jnp.concatenate([value[cut:, :], value[:cut, :]], axis=0)

    logs = [part[:, at : at + LANES].astype(BF16) for part in parts]
    for h in range(heads):
        pick = ((source == h) | (source == heads + h) | (source == 2 * heads + h)).astype(F32)
        pick = pick.astype(BF16)
        log = [
            turned(jnp.dot(c, pick, preferred_element_type=F32), i) for i, c in enumerate(logs)
        ]
        top = functools.reduce(jnp.maximum, log)
        weights = [jnp.exp2(value - top) for value in log]
        total = functools.reduce(jnp.add, weights)
        merged = functools.reduce(
            jnp.add,
            [
                w * turned(part[:, h * HEAD : (h + 1) * HEAD].astype(F32), i)
                for i, (w, part) in enumerate(zip(weights, parts))
            ],
        )
        merged = merged / total
        for begin, out in zip(starts, outs):
            out[:, h * HEAD : (h + 1) * HEAD] = merged[begin : begin + each, :].astype(out.dtype)
        if not last:
            hi, mid, lo = split3(top + jnp.log(total) * math.log2(math.e))
            columns = jnp.where(lane == h, hi, columns)
            columns = jnp.where(lane == heads + h, mid, columns)
            columns = jnp.where(lane == 2 * heads + h, lo, columns)
    if not last:
        for begin, out in zip(starts, outs):
            out[:, at : at + LANES] = columns[begin : begin + each, :].astype(out.dtype)


def merge(parts, rows, types, roll=False, last=False, name="merge"):
    width = parts[0].shape[1] - (LANES if last else 0)
    whole = pl.BlockSpec(memory_space=pltpu.VMEM)
    return pl.pallas_call(
        functools.partial(merge_kernel, len(parts), roll, last),
        in_specs=[whole] * len(parts),
        out_specs=[whole] * len(types),
        out_shape=[jax.ShapeDtypeStruct((rows, width), t) for t in types],
        compiler_params=pltpu.CompilerParams(vmem_limit_bytes=16 << 20),
        name=name,
    )(*parts)


def project_kernel(*refs):
    pieces, w, outs, whole = refs[:8], refs[8], refs[9:13], refs[13]
    rows = pieces[0].shape[0]
    attn = jnp.concatenate([piece[...] for piece in pieces], axis=0)
    product = jnp.dot(attn, w[...], preferred_element_type=F32)
    block = rows // 4
    host, z, x, core = place()
    tensor = lax.axis_index("tensor")
    for i in range(8):
        home_core = (core + i // 4) & 1
        home_z = z ^ (i % 4)
        for j in range(4):
            home_x = (x + 4 - j) & 3
            at = pl.multiple_of(((home_z * 4 + home_x) * 2 + home_core) * block, block)
            start = i * rows + j * block
            whole[pl.ds(at, block), :] = product[start : start + block, :]
    each = outs[0].shape[0]
    for ahead, out in enumerate(outs):
        at = pl.multiple_of(((tensor + ahead) & 3) * each, each)
        out[...] = whole[pl.ds(at, each), :]


def project(pieces, w):
    rows = 8 * pieces[0].shape[0]
    whole = pl.BlockSpec(memory_space=pltpu.VMEM)
    return pl.pallas_call(
        project_kernel,
        in_specs=[whole] * 9,
        out_specs=[whole] * 4,
        scratch_shapes=[pltpu.VMEM((rows, w.shape[1]), F32)],
        out_shape=[jax.ShapeDtypeStruct((rows // 4, w.shape[1]), F32)] * 4,
        compiler_params=pltpu.CompilerParams(vmem_limit_bytes=16 << 20),
        name="project",
    )(*pieces, w)


def host_at(z, x, core):
    return ((z % 4) * 4 + x % 4) * 2 + core


def moved(dz, dx, swap=0, cores=(0, 1)):
    return [
        (host_at(z, x, c), host_at(z + dz, x + dx, c ^ swap))
        for z in range(4)
        for x in range(4)
        for c in cores
    ]


def crossed(dz):
    return [
        (host_at(z, x, c), host_at(z ^ dz, x, c))
        for z in range(4)
        for x in range(4)
        for c in (0, 1)
    ]


def spread(steps):
    first = [(host_at(i, a, 0), host_at(i, b, 0)) for i in range(4) for a, b in steps]
    return first + [(host_at(a, i, 1), host_at(b, i, 1)) for i in range(4) for a, b in steps]


def send(value, perm):
    return lax.ppermute(value, "hst", perm)


def after(value, *others):
    return lax.optimization_barrier((value, *others))[0]


def shards(cq, ck, cv, qq, qk, qv, w, lengths):
    host, z, x, core = place()
    by_x = {d: send(qq, moved(0, d)) for d in (1, 3, 2)}
    vt = turn(cv)
    keys_or_values = jnp.where(core == 0, ck, send(vt.reshape(ck.shape), [(0, 1)]))
    row_q = jnp.concatenate([qq] + [after(by_x[d], vt) for d in (1, 2, 3)], axis=0)
    next_q = send(row_q, crossed(1))
    keys_or_values = after(keys_or_values, row_q)
    first_leg = {
        d: send(keys_or_values, [(0, host_at(d, 0, 0)), (1, host_at(0, d, 1))]) for d in (1, 3, 2)
    }
    tile1 = local_part(1, after(lengths, row_q, keys_or_values), cq, ck, vt)
    pair_q = jnp.concatenate([row_q, after(next_q, tile1[1])], axis=0)
    other_q = send(pair_q, crossed(2))
    along = jnp.where(core == 0, z, x)
    line = keys_or_values
    for d in (1, 3, 2):
        line = jnp.where(along == d, after(first_leg[d], tile1[1]), line)
    across = jnp.where(core == 0, x, z)
    third = send(line, spread([(0, 1)]))
    tile0 = local_part(0, after(lengths, line, pair_q), cq, ck, vt)
    far_q = send(pair_q, moved(0, 0, 1))
    other_q = after(other_q, tile0[1])
    pieces = [pair_q, other_q, after(far_q, tile0[1]), send(other_q, moved(0, 0, 1))]
    line = jnp.where(across == 1, after(third, tile0[1]), line)
    fourth = send(line, spread([(0, 3), (1, 2)]))
    near, far = query_part(after(lengths, line), pieces, ck, vt, qk, qv)
    other = send(far, moved(0, 0, 1))
    plane = jnp.where(across >= 2, after(fourth, near), line)
    swapped = send(plane, moved(0, 0, 1))
    dz = merge([near, other], near.shape[0] // 4, [F32, BF16, BF16, BF16], name="merge_core")
    from_z = [send(dz[d], crossed(d)) for d in (1, 3, 2)]
    anchor_k = jnp.where(core == 0, plane, swapped)
    anchor_vt = jnp.where(core == 0, swapped, plane).reshape(vt.shape)
    out = anchor_part(1, 0, 2, after(lengths, dz[0]), cq, anchor_k, anchor_vt, *tile1, None)
    own_q, mine_q = merge(
        [dz[0], *(after(p, out) for p in from_z)], dz[0].shape[0], [F32, BF16], name="merge_z"
    )
    from_x = [send(mine_q, moved(0, d)) for d in (1, 2, 3)]
    out = anchor_part(1, 2, 2, after(lengths, mine_q), cq, anchor_k, anchor_vt, *tile1, out)
    (attn,) = merge(
        [own_q, *(after(p, out) for p in from_x)], own_q.shape[0], [BF16], True, True, "merge_x"
    )
    others = [send(attn, crossed(d)) for d in (1, 2, 3)]
    out = anchor_part(0, 0, 2, after(lengths, attn), cq, anchor_k, anchor_vt, *tile0, out)
    attn_z = [attn] + [after(p, out) for p in others]
    attn_all = attn_z + [send(piece, moved(0, 0, 1)) for piece in attn_z]
    sums = project(attn_all, w)
    swaps = [
        lax.ppermute(sums[d], "tensor", [(i, (i + d) % 4) for i in range(4)]) for d in (1, 2, 3)
    ]
    out = anchor_part(0, 2, 2, after(lengths, sums[0]), cq, anchor_k, anchor_vt, *tile0, out)
    query_out = (sums[0] + swaps[0] + swaps[1] + swaps[2]).astype(BF16)
    return out, query_out


def solution(mesh):
    in_specs = (
        P("hst", "tensor"),
        P("hst", "tensor"),
        P("hst", "tensor"),
        P("hst", "tensor"),
        P("hst", "tensor"),
        P("hst", "tensor"),
        P("tensor", "hst"),
        P(),
    )
    out_specs = (P("hst", "tensor"), P("tensor", "hst"))
    return jax.shard_map(shards, mesh=mesh, in_specs=in_specs, out_specs=out_specs, check_vma=False)
```
